32 devices in a mesh: dp: 8 (over y, x, core), segment: 4 (over z).
Axes of the slice: x: 2, y: 2, z: 4, core: 2. Of those that a mesh axis runs over, the one named last changes fastest.
Arguments:
- inputs: bfloat16 [4, 8, 256, 1024], P('segment', 'dp'), may hold values from -6 to 6
- values: bfloat16 [4, 8, 256, 1024], P('segment', 'dp'), may hold values from -6 to 6
- gate_values: bfloat16 [4, 8, 256, 1024], P('segment', 'dp'), may hold values from -6 to 6
- out_grad: bfloat16 [4, 8, 256, 1024], P('segment', 'dp'), may hold values from -6 to 6
- lengths: int32 [4, 8], P('segment', 'dp'), may hold values from 32 to 256, as said below
- qk_weight: bfloat16 [4, 1024, 2048], P('segment', 'dp'), may hold values from -0.1875 to 0.1875
Outputs:
- grad_inputs: bfloat16 [4, 8, 256, 1024], P('segment', 'dp')
- grad_values: bfloat16 [4, 8, 256, 1024], P('segment', 'dp')
- grad_gates: bfloat16 [4, 8, 256, 1024], P('segment', 'dp')
- grad_weight: float32 [4, 1024, 2048], P('segment', 'dp')
The draws below stay inside these ranges and needn't reach their ends.
Inputs may be any that keep to these rules, and one draw needn't show every extreme that they name: `lengths`: in every layer some sequence has the full length 256.
All inputs are finite; a program needn't handle non-finite values.
Results may differ from the reference program's by a relative error of at most 0.025.
Values may be sent and summed in bfloat16 or wider, within the bound.
No kernel may reach another device: no remote copies, remote signals or barrier semaphores. Data moves between devices by JAX's collectives and lax.ppermute only.
A program may use at most 64 MiB of HBM per device.

```python
import jax
import jax.numpy as jnp
from jax import lax

D = 1024
H = 8
DH = 128
L = 256
LAYERS = 4
SEQS = 8


def draw_lengths(key, part):
    first_key, second_key = jax.random.split(jax.random.fold_in(key, 7))
    drawn = jax.random.randint(first_key, (LAYERS, SEQS), L // 8, L + 1)
    full_at = jax.random.randint(second_key, (LAYERS, 1), 0, SEQS)
    positions = jnp.arange(SEQS, dtype=jnp.int32)[None, :]
    return jnp.where(positions == full_at, L, drawn).astype(jnp.int32)


def raised(result, rng, source, target, blocks, factor):
    def block_of(dim):
        return (jnp.arange(result.shape[dim]) // (result.shape[dim] // blocks)).reshape((-1,) + (1,) * (result.ndim - 1 - dim))

    near = jax.random.permutation(rng, blocks)[block_of(target)]
    other_side = (block_of(target) + blocks // 2) % blocks
    return jnp.where((block_of(source) == near) | (block_of(source) == other_side), factor * result, result)


def block_levels(own_key, shape, pieces, least, high):
    gain = 1.0
    for dim, shards_of in pieces:
        steps = jax.random.uniform(jax.random.fold_in(jax.random.fold_in(own_key, 6), dim), (shards_of,), jnp.float32, least / len(pieces), high / len(pieces))
        gain = gain * jnp.repeat(jnp.exp(steps), shape[dim] // shards_of).reshape((-1,) + (1,) * (len(shape) - 1 - dim))
    return gain


def centred(key, dims, spread, most, pieces=(), kind=jnp.bfloat16):
    values = jax.random.normal(key, dims, jnp.float32) * spread
    if len(pieces) > 0:
        values = block_levels(key, dims, pieces, -0.22, 0.18) * values
    return jnp.clip(values, min=-most, max=most).astype(kind)


def heavy_noise(key, dims, deviation, bound, pieces, heavy, kind=jnp.bfloat16):
    values = deviation * jax.random.normal(key, dims, jnp.float32)
    if pieces:
        values = values * block_levels(key, dims, pieces, -0.22, 0.18)
    return jnp.clip(raised(values, jax.random.fold_in(key, 3), *heavy), -bound, bound).astype(kind)


def setup_inputs(seed: int = 0) -> dict:
    key_of = jax.random.split(jax.random.key(seed), 7)
    return {
        "inputs": heavy_noise(key_of[0], (LAYERS, SEQS, L, D), 1.0, 6.0, ((0, 4), (1, 8)), (1, 3, 8, 2.0)),
        "values": centred(key_of[1], (LAYERS, SEQS, L, H * DH), 1.0, 6.0, ((0, 4), (1, 8))),
        "gate_values": centred(key_of[2], (LAYERS, SEQS, L, H * DH), 1.0, 6.0, ((0, 4), (1, 8))),
        "out_grad": centred(key_of[3], (LAYERS, SEQS, L, D), 1.0, 6.0, ((0, 4), (1, 8))),
        "lengths": draw_lengths(jax.random.fold_in(key_of[6], 71), 0),
        "qk_weight": centred(key_of[5], (LAYERS, D, 2 * H * DH), D ** -0.5, 0.1875, ((0, 4), (1, 8))),
    }


def window(qk_pre, values, gate_values, length):
    seq_len = qk_pre.shape[0]
    qk_act = jax.nn.silu(qk_pre).astype(jnp.bfloat16)
    queries = qk_act[:, :H * DH].reshape(seq_len, H, DH).astype(jnp.float32)
    keys = qk_act[:, H * DH:].reshape(seq_len, H, DH).astype(jnp.float32)
    scores = jnp.einsum('ihd,jhd->hij', queries, keys) * DH ** (-0.5)
    row_ids = lax.broadcasted_iota(jnp.int32, (seq_len, seq_len), 0)
    col_ids = lax.broadcasted_iota(jnp.int32, (seq_len, seq_len), 1)
    valid = (col_ids <= row_ids) & (row_ids < length)
    attention = jnp.where(valid[None], jax.nn.silu(scores), 0.0).astype(jnp.bfloat16)
    heads_values = values.reshape(seq_len, H, DH).astype(jnp.float32)
    mixed_heads = jnp.einsum('hij,jhd->ihd', attention.astype(jnp.float32), heads_values).reshape(seq_len, H * DH)
    row_mean = lax.optimization_barrier(jnp.mean(mixed_heads, axis=-1, keepdims=True))
    centered = mixed_heads - row_mean
    variance = lax.optimization_barrier(jnp.mean(centered * centered, axis=-1, keepdims=True))
    normed = centered * lax.rsqrt(variance + 1e-05)
    live = (lax.broadcasted_iota(jnp.int32, (seq_len, 1), 0) < length).astype(jnp.float32)
    return normed * gate_values.astype(jnp.float32) * live

def reference(inputs, values, gate_values, out_grad, lengths, qk_weight):
    cotangents = jnp.roll(out_grad, -1, axis=0)

    def one_layer(layer_item):
        layer_in, layer_values, layer_gates, layer_cot, layer_len, weight = layer_item

        def one_seq(grad_total, seq_item):
            tokens_in, seq_values, seq_gates, seq_cot, length = seq_item
            pre = jnp.dot(tokens_in, weight, preferred_element_type=jnp.float32)
            outcome, pullback = jax.vjp(lambda a, b, c: window(a, b, c, length), pre, seq_values, seq_gates)
            grad_pre, grad_val, grad_gate = pullback(seq_cot.astype(jnp.float32))
            grad_pre_b = grad_pre.astype(jnp.bfloat16)
            grad_in = jnp.dot(grad_pre_b, weight.T, preferred_element_type=jnp.float32).astype(jnp.bfloat16)
            term = jnp.dot(tokens_in.T, grad_pre_b, preferred_element_type=jnp.float32)
            term_b = lax.optimization_barrier(term.astype(jnp.bfloat16))
            return (grad_total + term_b.astype(jnp.float32), (grad_in, grad_val, grad_gate))
        start_total = jnp.zeros(weight.shape, jnp.float32)
        grad_total, per_seq = lax.scan(one_seq, start_total, (layer_in, layer_values, layer_gates, layer_cot, layer_len))
        return (per_seq[0], per_seq[1], per_seq[2], grad_total)
    grad_inputs, grad_values, grad_gates, grad_weight = lax.map(one_layer, (inputs, values, gate_values, cotangents, lengths, qk_weight))
    return (grad_inputs, grad_values, grad_gates, grad_weight)
```

```python
import functools

import jax
import jax.numpy as jnp
from jax import lax
from jax.experimental import pallas as pl
from jax.experimental.pallas import tpu as pltpu
from jax.sharding import PartitionSpec as P

H = 8
DH = 128
F = H * DH
HALF = F // 2
HL = H // 2
SCALE = DH**-0.5
EPS = 1e-05
BF = jnp.bfloat16
F32 = jnp.float32
GROUPS = ((0, 1), (2, 3))

VMEM = pl.BlockSpec(memory_space=pltpu.VMEM)
SMEM = pl.BlockSpec(memory_space=pltpu.SMEM)


def pair(x, mask):
    count = lax.axis_size("dp")
    return lax.ppermute(x, "dp", [(i, i ^ mask) for i in range(count)])


def from_next(x, mask):
    dp, seg = lax.axis_size("dp"), lax.axis_size("segment")
    return lax.ppermute(
        x,
        ("dp", "segment"),
        [(i * seg + s, (i ^ mask) * seg + (s - 1) % seg) for i in range(dp) for s in range(seg)],
    )


def call(body, out_shape, *args, scratch=()):
    return pl.pallas_call(
        body,
        out_shape=out_shape,
        in_specs=[SMEM] + [VMEM] * (len(args) - 1),
        out_specs=jax.tree.map(lambda _: VMEM, out_shape),
        scratch_shapes=list(scratch),
        compiler_params=pltpu.CompilerParams(vmem_limit_bytes=48 << 20),
    )(*args)


def dot(a, b, ca, cb):
    return lax.dot_general(a, b, (((ca,), (cb,)), ((), ())), preferred_element_type=F32)


def ds(start, size, align):
    return pl.ds(pl.multiple_of(start, align), size)


def block_start(me, masks, rows):
    return lax.div(lax.bitwise_xor(me, masks[0]), len(masks)) * (len(masks) * rows)


def fill_block(me, masks, piece_refs, block):
    rows = piece_refs[0].shape[0]
    for m, ref in zip(masks, piece_refs):
        at = lax.rem(lax.bitwise_xor(me, m), len(masks)) * rows
        block[ds(at, rows, rows), :] = ref[...]


def turn_kernel(sc, xo, xp, xt):
    seq_len = xo.shape[0]
    xt[:, :seq_len] = xo[...].T
    xt[:, seq_len:] = xp[...].T


def pre_part(me, blocks, xo, xp, piece_refs, block, pre, add):
    rows = piece_refs[0].shape[0]
    seq_len = xo.shape[0]
    done = 0
    for masks in blocks:
        fill_block(me, masks, piece_refs[done : done + len(masks)], block)
        done += len(masks)
        cols = ds(block_start(me, masks, rows), len(masks) * rows, len(masks) * rows)
        for s, x in ((0, xo), (1, xp)):
            own = pl.ds(s * seq_len, seq_len)
            part = dot(x[:, cols], block[...], 1, 0)
            pre[own, :] = (pre[own, :] + part) if add else part
        add = True


def pre_kernel(blocks, has_prev, sc, xo, xp, *refs):
    me = sc[0]
    if has_prev:
        prev, refs = refs[0], refs[1:]
    *pieces, pre, block = refs
    if has_prev:
        pre[...] = prev[...]
    pre_part(me, blocks, xo, xp, pieces, block, pre, has_prev)


def forward_kernel(blocks, sc, xo, xp, prev, vo, vp, go, gp, co, cp, *refs):
    *pieces, act, slope, prob, dprob, mixed, stats, pre, block = refs
    me = sc[0]
    core = lax.rem(me, 2)
    seq_len = xo.shape[0]
    pre[...] = prev[...]
    pre_part(me, blocks, xo, xp, pieces, block, pre, True)
    row_ids = lax.broadcasted_iota(jnp.int32, (seq_len, seq_len), 0)
    col_ids = lax.broadcasted_iota(jnp.int32, (seq_len, seq_len), 1)
    for s in range(2):
        length = sc[1 + s]
        own = pl.ds(s * seq_len, seq_len)
        valid = (col_ids <= row_ids) & (row_ids < length)
        for h in range(HL):
            qk = []
            for side in range(2):
                at = pl.ds(side * HALF + h * DH, DH)
                v = pre[own, at]
                sig = 1.0 / (1.0 + jnp.exp(-v))
                a = (v * sig).astype(BF)
                act[own, at] = a
                slope[own, at] = sig * (1.0 + v * (1.0 - sig))
                qk.append(a)
            score = dot(qk[0], qk[1], 1, 1) * SCALE
            sig = 1.0 / (1.0 + jnp.exp(-score))
            p = jnp.where(valid, score * sig, 0.0).astype(BF)
            prob[s * HL + h] = p
            dprob[s * HL + h] = jnp.where(valid, sig * (1.0 + score * (1.0 - sig)) * SCALE, 0.0).astype(BF)
            if s == 0:
                val = vo[:, ds(core * HALF + h * DH, DH, DH)]
            else:
                val = vp[:, pl.ds(h * DH, DH)]
            mixed[own, pl.ds(h * DH, DH)] = dot(p, val, 1, 0)
        live = lax.broadcasted_iota(jnp.int32, (seq_len, 1), 0) < length
        if s == 0:
            gate = go[:, ds(core * HALF, HALF, HALF)]
            cot = co[...]
        else:
            gate = gp[...]
            cot = cp[...]
        grad = jnp.where(live, gate.astype(F32) * cot.astype(F32), 0.0)
        m = mixed[own, :]
        total = jnp.sum(m, axis=1, keepdims=True)
        off = m - total * (1.0 / HALF)
        cols = [
            total,
            jnp.sum(off * off, axis=1, keepdims=True),
            jnp.sum(grad, axis=1, keepdims=True),
            jnp.sum(grad * off, axis=1, keepdims=True),
        ]
        lane = lax.broadcasted_iota(jnp.int32, (seq_len, 128), 1)
        packed = jnp.zeros((seq_len, 128), F32)
        for i, col in enumerate(cols):
            packed = jnp.where(lane == i, col, packed)
        stats[:, own] = packed.T[:8, :]


def backward_kernel(heads, nmask, sc, xt, act, slope, prob, dprob, mixed, mine, theirs, vo, vp, go, gp, co, cp, *refs):
    *terms, gpre, gval, ggate, whole = refs
    me = sc[0]
    core = lax.rem(me, 2)
    seq_len = vo.shape[0]
    width = len(heads) * DH
    for s in range(2):
        length = sc[1 + s]
        own = pl.ds(s * seq_len, seq_len)
        other = pl.ds((1 - s) * seq_len, seq_len)
        mt = mine[:, own].T
        tt = theirs[:, other].T
        mean = (mt[:, 0:1] + tt[:, 0:1]) * (1.0 / F)
        mean_m = mt[:, 0:1] * (1.0 / HALF)
        mean_t = tt[:, 0:1] * (1.0 / HALF)
        gap = mean_m - mean_t
        variance = (mt[:, 1:2] + tt[:, 1:2] + gap * gap * (HALF * 0.5)) * (1.0 / F)
        rstd = lax.rsqrt(variance + EPS)
        c1 = (mt[:, 2:3] + tt[:, 2:3]) * (1.0 / F)
        cross = mt[:, 3:4] + tt[:, 3:4] + (mean_m - mean) * mt[:, 2:3] + (mean_t - mean) * tt[:, 2:3]
        c2 = cross * rstd * (1.0 / F)
        live = lax.broadcasted_iota(jnp.int32, (seq_len, 1), 0) < length
        for i, h in enumerate(heads):
            local = pl.ds(h * DH, DH)
            at = pl.ds(i * DH, DH)
            if s == 0:
                far = ds(core * HALF + h * DH, DH, DH)
                val, gate, cot = vo[:, far], go[:, far], co[:, local]
            else:
                val, gate, cot = vp[:, local], gp[:, local], cp[:, local]
            cot = cot.astype(F32)
            grad = jnp.where(live, gate.astype(F32) * cot, 0.0)
            normed = (mixed[own, local] - mean) * rstd
            ggate[own, at] = jnp.where(live, normed * cot, 0.0).astype(BF)
            dmix = (rstd * (grad - c1 - normed * c2)).astype(BF)
            q, k = act[own, local], act[own, pl.ds(HALF + h * DH, DH)]
            gval[own, at] = dot(prob[s * HL + h], dmix, 0, 0).astype(BF)
            datt = dot(dmix, val, 1, 1)
            dscore = (datt * dprob[s * HL + h].astype(F32)).astype(BF)
            dq = dot(dscore, k, 1, 0)
            dk = dot(dscore, q, 0, 0)
            gpre[own, at] = (dq * slope[own, local]).astype(BF)
            gpre[own, pl.ds(width + i * DH, DH)] = (dk * slope[own, pl.ds(HALF + h * DH, DH)]).astype(BF)
    whole[...] = dot(xt[...], gpre[...], 1, 0).astype(BF)
    rows = terms[0].shape[0]
    for m in range(nmask):
        terms[m][...] = whole[ds(lax.bitwise_xor(me, m) * rows, rows, rows), :]


def input_kernel(blocks, sc, *refs):
    *pieces, g0, g1, own_out, other_out, block = refs
    me = sc[0]
    rows = pieces[0].shape[0]
    seq_len = own_out.shape[0]
    width = g0.shape[1] // 2
    done = 0
    for masks in blocks:
        fill_block(me, masks, pieces[done : done + len(masks)], block)
        done += len(masks)
        cols = ds(block_start(me, masks, rows), len(masks) * rows, len(masks) * rows)
        for s, out in ((0, own_out), (1, other_out)):
            own = pl.ds(s * seq_len, seq_len)
            total = None
            for g, ref in enumerate((g0, g1)):
                for side in range(2):
                    part = dot(
                        ref[own, pl.ds(side * width, width)],
                        block[:, pl.ds(side * HALF + g * width, width)],
                        1,
                        1,
                    )
                    total = part if total is None else total + part
            out[:, cols] = total.astype(out.dtype)


def collect_kernel(sc, gi_o, gi_r, v0, v1, v0r, v1r, g0, g1, g0r, g1r, gi, gv, gg):
    core = lax.rem(sc[0], 2)
    seq_len = gi_o.shape[0]
    gi[...] = (gi_o[...] + gi_r[...].astype(F32)).astype(BF)
    for out, own, far in ((gv, (v0, v1), (v0r, v1r)), (gg, (g0, g1), (g0r, g1r))):
        for g in range(2):
            width = own[g].shape[1]
            out[:, ds(core * HALF + g * width, width, width)] = own[g][pl.ds(0, seq_len), :]
            out[:, ds((1 - core) * HALF + g * width, width, width)] = far[g][...]


def weight_kernel(sc, *refs):
    *parts, out = refs
    core = lax.rem(sc[0], 2)
    for g in range(2):
        own, far = parts[6 * g : 6 * g + 3], parts[6 * g + 3 : 6 * g + 6]
        width = own[0].shape[1] // 2
        for side in range(2):
            at = pl.ds(side * width, width)
            for c, three in ((core, own), (1 - core, far)):
                total = three[0][:, at].astype(F32) + three[1][:, at].astype(F32) + three[2][:, at].astype(F32)
                out[:, ds(side * F + c * HALF + g * width, width, width)] = total


def like(shape, kind):
    return jax.ShapeDtypeStruct(shape, kind)


def on_device(inputs, values, gate_values, out_grad, lengths, qk_weight):
    count = lax.axis_size("dp")
    me = lax.axis_index("dp")
    core = lax.rem(me, 2)
    xo, vo, go, grads = inputs[0, 0], values[0, 0], gate_values[0, 0], out_grad[0, 0]
    shard = qk_weight[0]
    rows, depth = shard.shape[0], xo.shape[1]
    seq_len = xo.shape[0]
    two = 2 * seq_len

    def half(x, c):
        return lax.dynamic_slice_in_dim(x, c * HALF, HALF, 1)

    low = jnp.concatenate([shard[:, :HALF], shard[:, F : F + HALF]], 1)
    high = jnp.concatenate([shard[:, HALF:F], shard[:, F + HALF :]], 1)
    mine = jnp.where(core == 0, low, high)
    other = jnp.where(core == 0, high, low)

    pieces = {0: mine}
    pieces[2] = pair(mine, 2)
    pieces[5] = pair(other, 5)
    pieces[1] = pair(other, 1)
    pieces[3] = pair(other, 3)
    pieces[4] = pair(mine, 4)
    pieces[6] = pair(pieces[2], 4)
    pieces[7] = pair(pieces[5], 2)
    bit = 8
    while bit < count:
        for m in range(bit):
            pieces[m + bit] = pair(pieces[m], bit)
        bit *= 2

    xp = pair(xo, 1)
    vp = pair(half(vo, 1 - core), 1)
    gp = pair(half(go, 1 - core), 1)
    co = from_next(half(grads, core), 0)
    cp = from_next(half(grads, 1 - core), 1)
    sc = jnp.concatenate([me.astype(jnp.int32)[None], lengths[0], pair(lengths[0], 1)])

    per = 256 // rows
    blocks = [tuple(range(b, b + per)) for b in range(0, count, per)]
    block = pltpu.VMEM((per * rows, F), BF)
    pre_shape = like((two, F), F32)

    def held(some):
        return [pieces[m] for masks in some for m in masks]

    xt = call(turn_kernel, like((depth, two), BF), sc, xo, xp)
    pre = call(
        functools.partial(pre_kernel, blocks[:1], False), pre_shape, sc, xo, xp, *held(blocks[:1]), scratch=[block]
    )
    pre = call(
        functools.partial(pre_kernel, blocks[1:-1], True),
        pre_shape,
        sc,
        xo,
        xp,
        pre,
        *held(blocks[1:-1]),
        scratch=[block],
    )
    act, slope, prob, dprob, mixed, stats = call(
        functools.partial(forward_kernel, blocks[-1:]),
        [
            like((two, F), BF),
            like((two, F), F32),
            like((2 * HL, seq_len, seq_len), BF),
            like((2 * HL, seq_len, seq_len), BF),
            like((two, HALF), F32),
            like((8, two), F32),
        ],
        sc,
        xo,
        xp,
        pre,
        vo,
        vp,
        go,
        gp,
        co,
        cp,
        *held(blocks[-1:]),
        scratch=[pltpu.VMEM((two, F), F32), block],
    )
    theirs = pair(stats, 1)

    gpre, gval, ggate, sums = [], [], [], []
    for heads in GROUPS:
        width = 2 * len(heads) * DH
        *terms, gpre_g, gval_g, ggate_g = call(
            functools.partial(backward_kernel, heads, count),
            [like((rows, width), BF)] * count
            + [like((two, width), BF), like((two, width // 2), BF), like((two, width // 2), BF)],
            sc,
            xt,
            act,
            slope,
            prob,
            dprob,
            mixed,
            stats,
            theirs,
            vo,
            vp,
            go,
            gp,
            co,
            cp,
            scratch=[pltpu.VMEM((depth, width), BF)],
        )
        gpre.append(gpre_g)
        gval.append(gval_g)
        ggate.append(ggate_g)
        bit = count // 2
        while bit >= 8:
            for m in range(bit):
                terms[m] = (terms[m].astype(F32) + pair(terms[m + bit], bit).astype(F32)).astype(BF)
            bit //= 2
        t4 = (terms[4].astype(F32) + pair(terms[6], 2).astype(F32)).astype(BF)
        t3 = (terms[3].astype(F32) + pair(terms[7], 4).astype(F32)).astype(BF)
        sums += [terms[0], pair(terms[2], 2), pair(t4, 4)]
        sums += [pair(terms[1], 1), pair(t3, 3), pair(terms[5], 5)]

    gi_o, gi_other = call(
        functools.partial(input_kernel, blocks),
        [like((seq_len, depth), F32), like((seq_len, depth), BF)],
        sc,
        *held(blocks),
        *gpre,
        scratch=[block],
    )
    grad_in, grad_val, grad_gate = call(
        collect_kernel,
        [like((seq_len, F), BF)] * 3,
        sc,
        gi_o,
        pair(gi_other, 1),
        *gval,
        *[pair(x[seq_len:], 1) for x in gval],
        *ggate,
        *[pair(x[seq_len:], 1) for x in ggate],
    )
    grad_shard = call(weight_kernel, like((rows, 2 * F), F32), sc, *sums)
    return (grad_in[None, None], grad_val[None, None], grad_gate[None, None], grad_shard[None])


def solution(mesh):
    return jax.shard_map(
        on_device,
        mesh=mesh,
        in_specs=(
            P("segment", "dp", None, None),
            P("segment", "dp", None, None),
            P("segment", "dp", None, None),
            P("segment", "dp", None, None),
            P("segment", "dp"),
            P("segment", "dp", None),
        ),
        out_specs=(
            P("segment", "dp", None, None),
            P("segment", "dp", None, None),
            P("segment", "dp", None, None),
            P("segment", "dp", None),
        ),
        check_vma=False,
    )
```

```python
import functools

import jax
import jax.numpy as jnp
from jax import lax
from jax.experimental import pallas as pl
from jax.experimental.pallas import tpu as pltpu
from jax.sharding import PartitionSpec as P

H = 8
DH = 128
F = H * DH
HALF = F // 2
HL = H // 2
SCALE = DH**-0.5
EPS = 1e-05
LOG2E = 1.4426950408889634
BF = jnp.bfloat16
F32 = jnp.float32
GROUPS = ((0, 1), (2, 3))

VMEM = pl.BlockSpec(memory_space=pltpu.VMEM)
SMEM = pl.BlockSpec(memory_space=pltpu.SMEM)


def pair(x, mask):
    count = lax.axis_size("dp")
    return lax.ppermute(x, "dp", [(i, i ^ mask) for i in range(count)])


def from_next(x, mask):
    dp, seg = lax.axis_size("dp"), lax.axis_size("segment")
    return lax.ppermute(
        x,
        ("dp", "segment"),
        [(i * seg + s, (i ^ mask) * seg + (s - 1) % seg) for i in range(dp) for s in range(seg)],
    )


def call(body, out_shape, *args, scratch=()):
    return pl.pallas_call(
        body,
        out_shape=out_shape,
        in_specs=[SMEM] + [VMEM] * (len(args) - 1),
        out_specs=jax.tree.map(lambda _: VMEM, out_shape),
        scratch_shapes=list(scratch),
        compiler_params=pltpu.CompilerParams(vmem_limit_bytes=20 << 20),
    )(*args)


def dot(a, b, ca, cb):
    return lax.dot_general(a, b, (((ca,), (cb,)), ((), ())), preferred_element_type=F32)


def ds(start, size, align):
    return pl.ds(pl.multiple_of(start, align), size)


def block_start(me, masks, rows):
    return lax.div(lax.bitwise_xor(me, masks[0]), len(masks)) * (len(masks) * rows)


def fill_block(me, masks, piece_refs, block):
    rows = piece_refs[0].shape[0]
    for m, ref in zip(masks, piece_refs):
        at = lax.rem(lax.bitwise_xor(me, m), len(masks)) * rows
        block[ds(at, rows, rows), :] = ref[...]


def turn_kernel(sc, xo, xp, xt):
    seq_len = xo.shape[0]
    xt[:, :seq_len] = xo[...].T
    xt[:, seq_len:] = xp[...].T


def pre_kernel(blocks, has_prev, sc, xo, xp, *refs):
    me = sc[0]
    if has_prev:
        prev, refs = refs[0], refs[1:]
    *pieces, pre, block = refs
    rows = pieces[0].shape[0]
    seq_len = xo.shape[0]
    for i, masks in enumerate(blocks):
        per = len(masks)
        fill_block(me, masks, pieces[i * per : (i + 1) * per], block)
        cols = ds(block_start(me, masks, rows), per * rows, per * rows)
        for s, x in ((0, xo), (1, xp)):
            own = pl.ds(s * seq_len, seq_len)
            part = dot(x[:, cols], block[...], 1, 0)
            if i > 0:
                part = part + pre[own, :]
            elif has_prev:
                part = part + prev[own, :]
            pre[own, :] = part


def gate(raw, scale):
    sig = pltpu.reciprocal(1.0 + jnp.exp2(raw * (-scale * LOG2E)), approx=True)
    out = raw * sig
    return out, sig + (out * scale if scale != 1.0 else out) * (1.0 - sig)


def product_kernel(sc, go, gp, co, cp, prod):
    core = lax.rem(sc[0], 2)
    seq_len = co.shape[0]
    prod[:seq_len, :] = go[:, ds(core * HALF, HALF, HALF)].astype(F32) * co[...].astype(F32)
    prod[seq_len:, :] = gp[...].astype(F32) * cp[...].astype(F32)


def forward_kernel(masks, sc, xo, xp, prev, vo, vp, prod, *refs):
    *pieces, act, slope, prob, dprob, mixed, stats, block = refs
    me = sc[0]
    core = lax.rem(me, 2)
    seq_len = xo.shape[0]
    top = seq_len // 2
    fill_block(me, masks, pieces, block)
    rows = pieces[0].shape[0]
    cols = ds(block_start(me, masks, rows), len(masks) * rows, len(masks) * rows)
    for s, x in ((0, xo), (1, xp)):
        own = pl.ds(s * seq_len, seq_len)
        a, d = gate(prev[own, :] + dot(x[:, cols], block[...], 1, 0), 1.0)
        act[own, :] = a.astype(BF)
        slope[own, :] = d
    causal = lax.broadcasted_iota(jnp.int32, (top, top), 1) <= lax.broadcasted_iota(jnp.int32, (top, top), 0)
    none = jnp.zeros((top, top), BF)
    units = [(s, h) for s in range(2) for h in range(HL)]
    raws = []
    for s, h in units:
        own = pl.ds(s * seq_len, seq_len)
        raws.append(dot(act[own, pl.ds(h * DH, DH)], act[own, pl.ds(HALF + h * DH, DH)], 1, 1))
    probs = []
    for (s, h), raw in zip(units, raws):
        p0, d0 = gate(raw[:top, :top], SCALE)
        p1, d1 = gate(raw[top:, :], SCALE)
        p0, d0 = jnp.where(causal, p0, 0.0), jnp.where(causal, d0, 0.0)
        p2, d2 = jnp.where(causal, p1[:, top:], 0.0), jnp.where(causal, d1[:, top:], 0.0)
        whole = []
        for upper, left, right in ((p0, p1, p2), (d0, d1, d2)):
            whole.append(
                jnp.concatenate(
                    [
                        jnp.concatenate([upper.astype(BF), none], 1),
                        jnp.concatenate([left[:, :top].astype(BF), right.astype(BF)], 1),
                    ],
                    0,
                )
            )
        probs.append(whole[0])
        prob[s * HL + h] = whole[0]
        dprob[s * HL + h] = whole[1]
    for (s, h), p in zip(units, probs):
        if s == 0:
            val = vo[:, ds(core * HALF + h * DH, DH, DH)]
        else:
            val = vp[:, pl.ds(h * DH, DH)]
        mixed[pl.ds(s * seq_len, seq_len), pl.ds(h * DH, DH)] = dot(p, val, 1, 0)
    for s in range(2):
        own = pl.ds(s * seq_len, seq_len)
        grad = prod[own, :]
        m = mixed[own, :]
        total = jnp.sum(m, axis=1, keepdims=True)
        off = m - total * (1.0 / HALF)
        cols = [
            total,
            jnp.sum(off * off, axis=1, keepdims=True),
            jnp.sum(grad, axis=1, keepdims=True),
            jnp.sum(grad * off, axis=1, keepdims=True),
        ]
        lane = lax.broadcasted_iota(jnp.int32, (seq_len, 128), 1)
        packed = jnp.zeros((seq_len, 128), F32)
        for i, col in enumerate(cols):
            packed = jnp.where(lane == i, col, packed)
        stats[:, own] = packed.T[:8, :]


def backward_kernel(heads, nmask, sc, xt, act, slope, prob, dprob, mixed, mine, theirs, vo, vp, prod, co, cp, *refs):
    *terms, gpre, gval, ggate, whole = refs
    me = sc[0]
    core = lax.rem(me, 2)
    seq_len = vo.shape[0]
    width = len(heads) * DH
    units = []
    for s in range(2):
        own = pl.ds(s * seq_len, seq_len)
        other = pl.ds((1 - s) * seq_len, seq_len)
        a, b = mine[:, own], theirs[:, other]
        mean = (a[0:1] + b[0:1]) * (1.0 / F)
        mean_a, mean_b = a[0:1] * (1.0 / HALF), b[0:1] * (1.0 / HALF)
        gap = mean_a - mean_b
        variance = (a[1:2] + b[1:2] + gap * gap * (HALF * 0.5)) * (1.0 / F)
        live = lax.broadcasted_iota(jnp.int32, (1, seq_len), 1) < sc[1 + s]
        rate = jnp.where(live, SCALE * lax.rsqrt(variance * (SCALE * SCALE) + EPS), 0.0)
        c1 = (a[2:3] + b[2:3]) * (1.0 / F)
        cross = a[3:4] + b[3:4] + (mean_a - mean) * a[2:3] + (mean_b - mean) * b[2:3]
        c2 = cross * rate * (1.0 / F)
        cols = jnp.concatenate([mean, rate, c1, c2, mean, rate, c1, c2], 0).T
        mean, rate, c1, c2 = (cols[:, i : i + 1] for i in range(4))
        for i, h in enumerate(heads):
            local = pl.ds(h * DH, DH)
            if s == 0:
                val, cot = vo[:, ds(core * HALF + h * DH, DH, DH)], co[:, local]
            else:
                val, cot = vp[:, local], cp[:, local]
            normed = (mixed[own, local] - mean) * rate
            ggate[own, pl.ds(i * DH, DH)] = (normed * cot.astype(F32)).astype(BF)
            dmix = (rate * (prod[own, local] - c1 - normed * c2)).astype(BF)
            units.append((own, i, h, s * HL + h, val, dmix))
    dscores = [dot(dmix, val, 1, 1).astype(BF) * dprob[u] for _, _, _, u, val, dmix in units]
    for (own, i, h, u, _, dmix), dscore in zip(units, dscores):
        gval[own, pl.ds(i * DH, DH)] = dot(prob[u], dmix, 0, 0).astype(BF)
        q_at, k_at = pl.ds(h * DH, DH), pl.ds(HALF + h * DH, DH)
        dq = dot(dscore, act[own, k_at], 1, 0)
        dk = dot(dscore, act[own, q_at], 0, 0)
        gpre[own, pl.ds(i * DH, DH)] = (dq * slope[own, q_at]).astype(BF)
        gpre[own, pl.ds(width + i * DH, DH)] = (dk * slope[own, k_at]).astype(BF)
    whole[...] = dot(xt[...], gpre[...], 1, 0).astype(BF)
    rows = terms[0].shape[0]
    for m in range(nmask):
        terms[m][...] = whole[ds(lax.bitwise_xor(me, m) * rows, rows, rows), :]


def input_kernel(blocks, sc, *refs):
    *pieces, g0, g1, own_out, other_out, block = refs
    me = sc[0]
    rows = pieces[0].shape[0]
    seq_len = own_out.shape[0]
    width = g0.shape[1] // 2
    done = 0
    for masks in blocks:
        fill_block(me, masks, pieces[done : done + len(masks)], block)
        done += len(masks)
        cols = ds(block_start(me, masks, rows), len(masks) * rows, len(masks) * rows)
        for s, out in ((0, own_out), (1, other_out)):
            own = pl.ds(s * seq_len, seq_len)
            total = None
            for g, ref in enumerate((g0, g1)):
                for side in range(2):
                    part = dot(
                        ref[own, pl.ds(side * width, width)],
                        block[:, pl.ds(side * HALF + g * width, width)],
                        1,
                        1,
                    )
                    total = part if total is None else total + part
            out[:, cols] = total.astype(out.dtype)


def collect_kernel(sc, gi_o, gi_r, v0, v1, v0r, v1r, g0, g1, g0r, g1r, gi, gv, gg):
    core = lax.rem(sc[0], 2)
    seq_len = gi_o.shape[0]
    gi[...] = (gi_o[...] + gi_r[...].astype(F32)).astype(BF)
    for out, own, far in ((gv, (v0, v1), (v0r, v1r)), (gg, (g0, g1), (g0r, g1r))):
        for g in range(2):
            width = own[g].shape[1]
            out[:, ds(core * HALF + g * width, width, width)] = own[g][pl.ds(0, seq_len), :]
            out[:, ds((1 - core) * HALF + g * width, width, width)] = far[g][...]


def weight_kernel(sc, *refs):
    *parts, out = refs
    core = lax.rem(sc[0], 2)
    for g in range(2):
        own, far = parts[6 * g : 6 * g + 3], parts[6 * g + 3 : 6 * g + 6]
        width = own[0].shape[1] // 2
        for side in range(2):
            at = pl.ds(side * width, width)
            for c, three in ((core, own), (1 - core, far)):
                total = three[0][:, at].astype(F32) + three[1][:, at].astype(F32) + three[2][:, at].astype(F32)
                out[:, ds(side * F + c * HALF + g * width, width, width)] = total


def like(shape, kind):
    return jax.ShapeDtypeStruct(shape, kind)


def on_device(inputs, values, gate_values, out_grad, lengths, qk_weight):
    count = lax.axis_size("dp")
    me = lax.axis_index("dp")
    core = lax.rem(me, 2)
    xo, vo, go, grads = inputs[0, 0], values[0, 0], gate_values[0, 0], out_grad[0, 0]
    shard = qk_weight[0]
    rows, depth = shard.shape[0], xo.shape[1]
    seq_len = xo.shape[0]
    two = 2 * seq_len

    def half(x, c):
        return lax.dynamic_slice_in_dim(x, c * HALF, HALF, 1)

    low = jnp.concatenate([shard[:, :HALF], shard[:, F : F + HALF]], 1)
    high = jnp.concatenate([shard[:, HALF:F], shard[:, F + HALF :]], 1)
    mine = jnp.where(core == 0, low, high)
    other = jnp.where(core == 0, high, low)

    pieces = {0: mine}
    pieces[2] = pair(mine, 2)
    pieces[5] = pair(other, 5)
    pieces[1] = pair(other, 1)
    pieces[3] = pair(other, 3)
    pieces[4] = pair(mine, 4)
    pieces[6] = pair(pieces[2], 4)
    pieces[7] = pair(pieces[5], 2)
    bit = 8
    while bit < count:
        for m in range(bit):
            pieces[m + bit] = pair(pieces[m], bit)
        bit *= 2

    xp = pair(xo, 1)
    vp = pair(half(vo, 1 - core), 1)
    gp = pair(half(go, 1 - core), 1)
    co = from_next(half(grads, core), 0)
    cp = from_next(half(grads, 1 - core), 1)
    sc = jnp.concatenate([me.astype(jnp.int32)[None], lengths[0], pair(lengths[0], 1)])

    per = 256 // rows
    blocks = [tuple(range(b, b + per)) for b in range(0, count, per)]
    block = pltpu.VMEM((per * rows, F), BF)
    pre_shape = like((two, F), F32)

    def held(some):
        return [pieces[m] for masks in some for m in masks]

    xt = call(turn_kernel, like((depth, two), BF), sc, xo, xp)
    pre = call(
        functools.partial(pre_kernel, blocks[:1], False), pre_shape, sc, xo, xp, *held(blocks[:1]), scratch=[block]
    )
    pre = call(
        functools.partial(pre_kernel, blocks[1:-1], True),
        pre_shape,
        sc,
        xo,
        xp,
        pre,
        *held(blocks[1:-1]),
        scratch=[block],
    )
    prod = call(product_kernel, like((two, HALF), F32), sc, go, gp, co, cp)
    act, slope, prob, dprob, mixed, stats = call(
        functools.partial(forward_kernel, blocks[-1]),
        [
            like((two, F), BF),
            like((two, F), F32),
            like((2 * HL, seq_len, seq_len), BF),
            like((2 * HL, seq_len, seq_len), BF),
            like((two, HALF), F32),
            like((8, two), F32),
        ],
        sc,
        xo,
        xp,
        pre,
        vo,
        vp,
        prod,
        *held(blocks[-1:]),
        scratch=[block],
    )
    theirs = pair(stats, 1)

    gpre, gval, ggate, sums = [], [], [], []
    for heads in GROUPS:
        width = 2 * len(heads) * DH
        *terms, gpre_g, gval_g, ggate_g = call(
            functools.partial(backward_kernel, heads, count),
            [like((rows, width), BF)] * count
            + [like((two, width), BF), like((two, width // 2), BF), like((two, width // 2), BF)],
            sc,
            xt,
            act,
            slope,
            prob,
            dprob,
            mixed,
            stats,
            theirs,
            vo,
            vp,
            prod,
            co,
            cp,
            scratch=[pltpu.VMEM((depth, width), BF)],
        )
        gpre.append(gpre_g)
        gval.append(gval_g)
        ggate.append(ggate_g)
        bit = count // 2
        while bit >= 8:
            for m in range(bit):
                terms[m] = (terms[m].astype(F32) + pair(terms[m + bit], bit).astype(F32)).astype(BF)
            bit //= 2
        t4 = (terms[4].astype(F32) + pair(terms[6], 2).astype(F32)).astype(BF)
        t3 = (terms[3].astype(F32) + pair(terms[7], 4).astype(F32)).astype(BF)
        sums += [terms[0], pair(terms[2], 2), pair(t4, 4)]
        sums += [pair(terms[1], 1), pair(t3, 3), pair(terms[5], 5)]

    gi_o, gi_other = call(
        functools.partial(input_kernel, blocks),
        [like((seq_len, depth), F32), like((seq_len, depth), BF)],
        sc,
        *held(blocks),
        *gpre,
        scratch=[block],
    )
    grad_in, grad_val, grad_gate = call(
        collect_kernel,
        [like((seq_len, F), BF)] * 3,
        sc,
        gi_o,
        pair(gi_other, 1),
        *gval,
        *[pair(x[seq_len:], 1) for x in gval],
        *ggate,
        *[pair(x[seq_len:], 1) for x in ggate],
    )
    grad_shard = call(weight_kernel, like((rows, 2 * F), F32), sc, *sums)
    return (grad_in[None, None], grad_val[None, None], grad_gate[None, None], grad_shard[None])


def solution(mesh):
    return jax.shard_map(
        on_device,
        mesh=mesh,
        in_specs=(
            P("segment", "dp", None, None),
            P("segment", "dp", None, None),
            P("segment", "dp", None, None),
            P("segment", "dp", None, None),
            P("segment", "dp"),
            P("segment", "dp", None),
        ),
        out_specs=(
            P("segment", "dp", None, None),
            P("segment", "dp", None, None),
            P("segment", "dp", None, None),
            P("segment", "dp", None),
        ),
        check_vma=False,
    )
```

```python
import functools

import jax
import jax.numpy as jnp
from jax import lax
from jax.experimental import pallas as pl
from jax.experimental.pallas import tpu as pltpu
from jax.sharding import PartitionSpec as P

H = 8
DH = 128
F = H * DH
HALF = F // 2
HL = H // 2
SCALE = DH**-0.5
EPS = 1e-05
LOG2E = 1.4426950408889634
BF = jnp.bfloat16
F32 = jnp.float32
UNIT = 1e9

VMEM = pl.BlockSpec(memory_space=pltpu.VMEM)
SMEM = pl.BlockSpec(memory_space=pltpu.SMEM)


def pair(x, mask):
    count = lax.axis_size("dp")
    return lax.ppermute(x, "dp", [(i, i ^ mask) for i in range(count)])


def from_next(x, mask=0):
    dp, seg = lax.axis_size("dp"), lax.axis_size("segment")
    return lax.ppermute(
        x,
        ("dp", "segment"),
        [(i * seg + s, (i ^ mask) * seg + (s - 1) % seg) for i in range(dp) for s in range(seg)],
    )


def call(body, cost, out_shape, *args, scratch=()):
    return pl.pallas_call(
        body,
        out_shape=out_shape,
        in_specs=[SMEM if x.dtype == jnp.int32 else VMEM for x in args],
        out_specs=jax.tree.map(lambda _: VMEM, out_shape),
        scratch_shapes=list(scratch),
        cost_estimate=pl.CostEstimate(flops=int(cost * UNIT), bytes_accessed=int(cost * UNIT), transcendentals=0),
        compiler_params=pltpu.CompilerParams(vmem_limit_bytes=20 << 20),
    )(*args)


def dot(a, b, ca, cb):
    return lax.dot_general(a, b, (((ca,), (cb,)), ((), ())), preferred_element_type=F32)


def ds(start, size, align):
    return pl.ds(pl.multiple_of(start, align), size)


def after(x, *deps):
    return lax.optimization_barrier((x, *deps))[0]


def block_start(me, masks, rows):
    return lax.div(lax.bitwise_xor(me, masks[0]), len(masks)) * (len(masks) * rows)


def fill_block(me, masks, piece_refs, block):
    rows = piece_refs[0].shape[0]
    for m, ref in zip(masks, piece_refs):
        at = lax.rem(lax.bitwise_xor(me, m), len(masks)) * rows
        block[ds(at, rows, rows), :] = ref[...]


def pack_kernel(x, values, gates, x_copy, mine, other):
    core = lax.rem(lax.axis_index("dp"), 2)
    x_copy[...] = x[...]
    for i, ref in enumerate((values, gates)):
        at = pl.ds(i * HALF, HALF)
        mine[:, at] = ref[:, ds(core * HALF, HALF, HALF)]
        other[:, at] = ref[:, ds((1 - core) * HALF, HALF, HALF)]


def turn_kernel(count, xo, xp, xt, natural):
    seq_len, depth = xo.shape
    rows = depth // count
    natural[:, :seq_len] = xo[...].T
    natural[:, seq_len:] = xp[...].T
    for m in range(count):
        xt[m * rows : (m + 1) * rows, :] = natural[ds(lax.bitwise_xor(lax.axis_index("dp"), m) * rows, rows, rows), :]


def pre_kernel(blocks, has_prev, xo, xp, *refs):
    me = lax.axis_index("dp")
    if has_prev:
        prev, refs = refs[0], refs[1:]
    *pieces, pre, block = refs
    rows = pieces[0].shape[0]
    seq_len = xo.shape[0]
    for i, masks in enumerate(blocks):
        per = len(masks)
        fill_block(me, masks, pieces[i * per : (i + 1) * per], block)
        cols = ds(block_start(me, masks, rows), per * rows, per * rows)
        for s, x in ((0, xo), (1, xp)):
            own = pl.ds(s * seq_len, seq_len)
            part = dot(x[:, cols], block[...], 1, 0)
            if i > 0:
                part = part + pre[own, :]
            elif has_prev:
                part = part + prev[own, :]
            pre[own, :] = part


def gate(raw, scale):
    sig = pltpu.reciprocal(1.0 + jnp.exp2(raw * (-scale * LOG2E)), approx=True)
    out = raw * sig
    return out, sig + (out * scale if scale != 1.0 else out) * (1.0 - sig)


def forward_kernel(masks, xo, xp, prev, vgo, vgp, *refs):
    *pieces, act, slope, prob, dprob, mixed, block = refs
    me = lax.axis_index("dp")
    seq_len = xo.shape[0]
    top = seq_len // 2
    fill_block(me, masks, pieces, block)
    rows = pieces[0].shape[0]
    cols = ds(block_start(me, masks, rows), len(masks) * rows, len(masks) * rows)
    for s, x in ((0, xo), (1, xp)):
        own = pl.ds(s * seq_len, seq_len)
        a, d = gate(prev[own, :] + dot(x[:, cols], block[...], 1, 0), 1.0)
        act[own, :] = a.astype(BF)
        slope[own, :] = d
    causal = lax.broadcasted_iota(jnp.int32, (top, top), 1) <= lax.broadcasted_iota(jnp.int32, (top, top), 0)
    none = jnp.zeros((top, top), BF)
    units = [(s, h) for s in range(2) for h in range(HL)]
    raws = []
    for s, h in units:
        own = pl.ds(s * seq_len, seq_len)
        raws.append(dot(act[own, pl.ds(h * DH, DH)], act[own, pl.ds(HALF + h * DH, DH)], 1, 1))
    probs = []
    for (s, h), raw in zip(units, raws):
        p0, d0 = gate(raw[:top, :top], SCALE)
        p1, d1 = gate(raw[top:, :], SCALE)
        p0, d0 = jnp.where(causal, p0, 0.0), jnp.where(causal, d0, 0.0)
        p2, d2 = jnp.where(causal, p1[:, top:], 0.0), jnp.where(causal, d1[:, top:], 0.0)
        whole = []
        for upper, left, right in ((p0, p1, p2), (d0, d1, d2)):
            whole.append(
                jnp.concatenate(
                    [
                        jnp.concatenate([upper.astype(BF), none], 1),
                        jnp.concatenate([left[:, :top].astype(BF), right.astype(BF)], 1),
                    ],
                    0,
                )
            )
        probs.append(whole[0])
        prob[s * HL + h] = whole[0]
        dprob[s * HL + h] = whole[1]
    for (s, h), p in zip(units, probs):
        val = (vgp if s else vgo)[:, pl.ds(h * DH, DH)]
        mixed[pl.ds(s * seq_len, seq_len), pl.ds(h * DH, DH)] = dot(p, val, 1, 0)


def stats_kernel(length, mixed, vgo, vgp, co, cp, prod, stats):
    seq_len = co.shape[0]
    prod[:seq_len, :] = vgo[:, HALF:].astype(F32) * co[...].astype(F32)
    prod[seq_len:, :] = vgp[:, HALF:].astype(F32) * cp[...].astype(F32)
    lane = lax.broadcasted_iota(jnp.int32, (seq_len, 128), 1)
    row = lax.broadcasted_iota(jnp.int32, (seq_len, 128), 0)
    live = jnp.where(row < length[0, 0], 1.0, 0.0)
    for s in range(2):
        own = pl.ds(s * seq_len, seq_len)
        grad = prod[own, :]
        m = mixed[own, :]
        total = jnp.sum(m, axis=1, keepdims=True)
        off = m - total * (1.0 / HALF)
        cols = [
            total,
            jnp.sum(off * off, axis=1, keepdims=True),
            jnp.sum(grad, axis=1, keepdims=True),
            jnp.sum(grad * off, axis=1, keepdims=True),
        ]
        packed = live
        for i, col in enumerate(cols):
            packed = jnp.where(lane == i, col, packed)
        stats[:, own] = packed.T[:8, :]


def backward_kernel(far, xt, act, slope, prob, dprob, mixed, mine, theirs, vgo, vgp, prod, co, cp, *refs):
    gpre, own_grads, far_grads, *terms = refs
    seq_len = co.shape[0]
    grad_refs = own_grads, far_grads
    units = []
    for s in range(2):
        own = pl.ds(s * seq_len, seq_len)
        other = pl.ds((1 - s) * seq_len, seq_len)
        a, b = mine[:, own], theirs[:, other]
        mean = (a[0:1] + b[0:1]) * (1.0 / F)
        mean_a, mean_b = a[0:1] * (1.0 / HALF), b[0:1] * (1.0 / HALF)
        gap = mean_a - mean_b
        variance = (a[1:2] + b[1:2] + gap * gap * (HALF * 0.5)) * (1.0 / F)
        live = (b if s else a)[4:5] > 0.5
        rate = jnp.where(live, SCALE * lax.rsqrt(variance * (SCALE * SCALE) + EPS), 0.0)
        c1 = (a[2:3] + b[2:3]) * (1.0 / F)
        cross = a[3:4] + b[3:4] + (mean_a - mean) * a[2:3] + (mean_b - mean) * b[2:3]
        c2 = cross * rate * (1.0 / F)
        cols = jnp.concatenate([mean, rate, c1, c2, mean, rate, c1, c2], 0).T
        mean, rate, c1, c2 = (cols[:, i : i + 1] for i in range(4))
        for h in range(HL):
            local = pl.ds(h * DH, DH)
            val, cot = (vgp[:, local], cp[:, local]) if s else (vgo[:, local], co[:, local])
            normed = (mixed[own, local] - mean) * rate
            grad_refs[s][:, pl.ds(HALF + h * DH, DH)] = (normed * cot.astype(F32)).astype(BF)
            dmix = (rate * (prod[own, local] - c1 - normed * c2)).astype(BF)
            units.append((own, h, s * HL + h, val, dmix))
    dscores = [dot(dmix, val, 1, 1).astype(BF) * dprob[u] for _, _, u, val, dmix in units]
    for (own, h, u, _, dmix), dscore in zip(units, dscores):
        grad_refs[u // HL][:, pl.ds(h * DH, DH)] = dot(prob[u], dmix, 0, 0).astype(BF)
        q_at, k_at = pl.ds(h * DH, DH), pl.ds(HALF + h * DH, DH)
        dq = dot(dscore, act[own, k_at], 1, 0)
        dk = dot(dscore, act[own, q_at], 0, 0)
        gpre[own, q_at] = (dq * slope[own, q_at]).astype(BF)
        gpre[own, k_at] = (dk * slope[own, k_at]).astype(BF)
    rows = terms[0].shape[0]
    for m, term in zip(far, terms):
        term[...] = dot(xt[m * rows : (m + 1) * rows, :], gpre[...], 1, 0).astype(BF)


def term_kernel(near, xt, gpre, *terms):
    rows = terms[0].shape[0]
    for first in range(0, len(near), 2):
        m = near[first]
        both = dot(xt[m * rows : (m + 2) * rows, :], gpre[...], 1, 0).astype(BF)
        terms[first][...] = both[:rows, :]
        terms[first + 1][...] = both[rows:, :]


def fold_kernel(first, added, out):
    out[...] = (first[...].astype(F32) + added[...].astype(F32)).astype(BF)


def near_kernel(own, x, far, y, out_own, out_far):
    out_own[...] = own[...].astype(F32) + x[...].astype(F32)
    out_far[...] = far[...].astype(F32) + y[...].astype(F32)


def input_kernel(blocks, *refs):
    *pieces, gpre, own_out, other_out, block = refs
    me = lax.axis_index("dp")
    rows = pieces[0].shape[0]
    seq_len = own_out.shape[0]
    done = 0
    for masks in blocks:
        fill_block(me, masks, pieces[done : done + len(masks)], block)
        done += len(masks)
        cols = ds(block_start(me, masks, rows), len(masks) * rows, len(masks) * rows)
        for s, out in ((0, own_out), (1, other_out)):
            out[:, cols] = dot(gpre[pl.ds(s * seq_len, seq_len), :], block[...], 1, 1).astype(out.dtype)


def collect_kernel(gi_o, gi_r, own, far, gi, gv, gg):
    core = lax.rem(lax.axis_index("dp"), 2)
    gi[...] = (gi_o[...] + gi_r[...].astype(F32)).astype(BF)
    for c, ref in ((core, own), (1 - core, far)):
        for i, out in enumerate((gv, gg)):
            out[:, ds(c * HALF, HALF, HALF)] = ref[:, pl.ds(i * HALF, HALF)]


def weight_kernel(own, x, far, y, out):
    core = lax.rem(lax.axis_index("dp"), 2)
    for c, near, added in ((core, own, x), (1 - core, far, y)):
        for side in range(2):
            at = pl.ds(side * HALF, HALF)
            out[:, ds(side * F + c * HALF, HALF, HALF)] = near[:, at] + added[:, at].astype(F32)


def like(shape, kind):
    return jax.ShapeDtypeStruct(shape, kind)


def halve(terms, count):
    bit = count // 2
    while bit >= 8:
        terms = {
            m: (t.astype(F32) + pair(terms[m + bit], bit).astype(F32)).astype(BF) for m, t in terms.items() if m < bit
        }
        bit //= 2
    return terms


def on_device(inputs, values, gate_values, out_grad, lengths, qk_weight):
    count = lax.axis_size("dp")
    core = lax.rem(lax.axis_index("dp"), 2)
    xo, vo, go, grads = inputs[0, 0], values[0, 0], gate_values[0, 0], out_grad[0, 0]
    shard = qk_weight[0]
    rows, depth = shard.shape[0], xo.shape[1]
    seq_len = xo.shape[0]
    two = 2 * seq_len
    per = 256 // rows
    blocks = [tuple(range(b, b + per)) for b in range(0, count, per)]
    block = pltpu.VMEM((per * rows, F), BF)

    def half(x, c):
        return lax.dynamic_slice_in_dim(x, c * HALF, HALF, 1)

    def held(some):
        return [pieces[m] for masks in some for m in masks]

    low = jnp.concatenate([shard[:, :HALF], shard[:, F : F + HALF]], 1)
    high = jnp.concatenate([shard[:, HALF:F], shard[:, F + HALF :]], 1)
    mine = jnp.where(core == 0, low, high)
    other = jnp.where(core == 0, high, low)
    pieces = {0: mine}
    pieces[1] = pair(other, 1)
    pieces[2] = pair(mine, 2)
    pieces[5] = pair(other, 5)
    xp = pair(after(xo, mine), 1)
    xo, vgo, vgp = call(pack_kernel, 0.001, [like((seq_len, F), BF)] * 3, xo, vo, go)
    cp = from_next(half(after(grads, pieces[1]), 1 - core), 1)
    co = from_next(half(after(grads, pieces[1]), core))
    vgp = pair(vgp, 1)
    pieces[3] = pair(after(other, xp, pieces[1], vgp), 3)
    pieces[4] = pair(after(mine, xp, pieces[1], vgp), 4)

    xt = call(
        functools.partial(turn_kernel, count),
        10,
        like((depth, two), BF),
        xo,
        xp,
        scratch=[pltpu.VMEM((depth, two), BF)],
    )
    pieces[6] = pair(pieces[2], 4)
    pieces[7] = pair(pieces[5], 2)
    bit = 8
    while bit < count:
        for m in range(bit):
            pieces[m + bit] = pair(pieces[m], bit)
        bit *= 2
    first = functools.partial(pre_kernel, blocks[:1], False)
    pre = call(first, 0.001, like((two, F), F32), xo, xp, *held(blocks[:1]), scratch=[block])
    more = functools.partial(pre_kernel, blocks[1:-1], True)
    pre = call(more, 0.001, like((two, F), F32), xo, xp, pre, *held(blocks[1:-1]), scratch=[block])
    cp, pre = lax.optimization_barrier((cp, pre))
    act, slope, prob, dprob, mixed = call(
        functools.partial(forward_kernel, blocks[-1]),
        0.001,
        [
            like((two, F), BF),
            like((two, F), F32),
            like((2 * HL, seq_len, seq_len), BF),
            like((2 * HL, seq_len, seq_len), BF),
            like((two, HALF), F32),
        ],
        xo,
        xp,
        pre,
        vgo,
        vgp,
        *held(blocks[-1:]),
        scratch=[block],
    )
    prod, stats = call(
        stats_kernel,
        1, [like((two, HALF), F32), like((8, two), F32)], lengths, mixed, vgo, vgp, co, cp
    )
    theirs = pair(stats, 1)

    far = [m for m in range(count) if m % 8 >= 6]
    near = [m for m in range(count) if m % 8 < 6]
    gpre, own_g, far_g, *terms = call(
        functools.partial(backward_kernel, far),
        0.1,
        [like((two, F), BF)] + [like((seq_len, F), BF)] * 2 + [like((rows, F), BF)] * len(far),
        xt,
        act,
        slope,
        prob,
        dprob,
        mixed,
        stats,
        theirs,
        vgo,
        vgp,
        prod,
        co,
        cp,
    )
    diagonal = halve(dict(zip(far, terms)), count)
    far_g = pair(far_g, 1)
    by_x, by_y = lax.optimization_barrier((pair(diagonal[6], 2), pair(diagonal[7], 4)))
    terms = call(functools.partial(term_kernel, near), 0.1, [like((rows, F), BF)] * len(near), xt, gpre)
    t = halve(dict(zip(near, terms)), count)
    x_r, y_r = lax.optimization_barrier((pair(t[2], 2), pair(t[5], 5)))
    far_t = pair(after(t[1], far_g), 1)
    near_own, near_far = call(near_kernel, 0.001, [like((rows, F), F32)] * 2, t[0], x_r, far_t, y_r)
    gi_o, gi_other = call(
        functools.partial(input_kernel, blocks),
        10,
        [like((seq_len, depth), F32), like((seq_len, depth), BF)],
        *held(blocks),
        gpre,
        scratch=[block],
    )
    gi_r = pair(after(gi_other, far_t), 1)
    send_y = call(fold_kernel, 0.3, like((rows, F), BF), t[4], by_x)
    send_x = call(fold_kernel, 0.3, like((rows, F), BF), t[3], by_y)
    grad_in, grad_val, grad_gate = call(
        collect_kernel, 0.3, [like((seq_len, F), BF)] * 3, gi_o, gi_r, own_g, far_g
    )
    sums = [near_own, pair(send_y, 4), near_far, pair(send_x, 3)]
    sums, _ = lax.optimization_barrier((sums, (grad_in, grad_val, grad_gate)))
    grad_shard = call(weight_kernel, 1, like((rows, 2 * F), F32), *sums)
    return (grad_in[None, None], grad_val[None, None], grad_gate[None, None], grad_shard[None])


def solution(mesh):
    return jax.shard_map(
        on_device,
        mesh=mesh,
        in_specs=(
            P("segment", "dp", None, None),
            P("segment", "dp", None, None),
            P("segment", "dp", None, None),
            P("segment", "dp", None, None),
            P("segment", "dp"),
            P("segment", "dp", None),
        ),
        out_specs=(
            P("segment", "dp", None, None),
            P("segment", "dp", None, None),
            P("segment", "dp", None, None),
            P("segment", "dp", None),
        ),
        check_vma=False,
    )
```

```python
import functools

import jax
import jax.numpy as jnp
from jax import lax
from jax.experimental import pallas as pl
from jax.experimental.pallas import tpu as pltpu
from jax.sharding import PartitionSpec as P

H = 8
DH = 128
F = H * DH
HALF = F // 2
HL = H // 2
SCALE = DH**-0.5
EPS = 1e-05
LOG2E = 1.4426950408889634
BF = jnp.bfloat16
F32 = jnp.float32
UNIT = 1e9

VMEM = pl.BlockSpec(memory_space=pltpu.VMEM)
SMEM = pl.BlockSpec(memory_space=pltpu.SMEM)


def pair(x, mask):
    count = lax.axis_size("dp")
    return lax.ppermute(x, "dp", [(i, i ^ mask) for i in range(count)])


def from_next(x, mask=0):
    dp, seg = lax.axis_size("dp"), lax.axis_size("segment")
    return lax.ppermute(
        x,
        ("dp", "segment"),
        [(i * seg + s, (i ^ mask) * seg + (s - 1) % seg) for i in range(dp) for s in range(seg)],
    )


def call(body, cost, out_shape, *args, scratch=()):
    return pl.pallas_call(
        body,
        out_shape=out_shape,
        in_specs=[SMEM if x.dtype == jnp.int32 else VMEM for x in args],
        out_specs=jax.tree.map(lambda _: VMEM, out_shape),
        scratch_shapes=list(scratch),
        cost_estimate=pl.CostEstimate(flops=int(cost * UNIT), bytes_accessed=int(cost * UNIT), transcendentals=0),
        compiler_params=pltpu.CompilerParams(vmem_limit_bytes=20 << 20),
    )(*args)


def dot(a, b, ca, cb):
    return lax.dot_general(a, b, (((ca,), (cb,)), ((), ())), preferred_element_type=F32)


def ds(start, size, align):
    return pl.ds(pl.multiple_of(start, align), size)


def after(x, *deps):
    return lax.optimization_barrier((x, *deps))[0]


def block_start(me, masks, rows):
    return lax.div(lax.bitwise_xor(me, masks[0]), len(masks)) * (len(masks) * rows)


def fill_block(me, masks, piece_refs, block):
    rows = piece_refs[0].shape[0]
    for m, ref in zip(masks, piece_refs):
        at = lax.rem(lax.bitwise_xor(me, m), len(masks)) * rows
        block[ds(at, rows, rows), :] = ref[...]


def pack_kernel(other, x, values, gates, bundle, vg):
    core = lax.rem(lax.axis_index("dp"), 2)
    seq_len, rows = x.shape[0], other.shape[0]
    bundle[:seq_len, :] = x[...]
    bundle[pl.ds(2 * seq_len, rows), :] = other[...]
    for i, ref in enumerate((values, gates)):
        at = pl.ds(i * HALF, HALF)
        vg[:, at] = ref[:, ds(core * HALF, HALF, HALF)]
        bundle[pl.ds(seq_len, seq_len), at] = ref[:, ds((1 - core) * HALF, HALF, HALF)]


def turn_kernel(count, bo, bp, xt, natural):
    depth, seq_len = xt.shape[0], xt.shape[1] // 2
    rows = depth // count
    natural[:, :seq_len] = bo[:seq_len, :].T
    natural[:, seq_len:] = bp[:seq_len, :].T
    for m in range(count):
        xt[m * rows : (m + 1) * rows, :] = natural[ds(lax.bitwise_xor(lax.axis_index("dp"), m) * rows, rows, rows), :]


def pre_kernel(blocks, has_prev, bo, bp, *refs):
    me = lax.axis_index("dp")
    if has_prev:
        prev, refs = refs[0], refs[1:]
    *pieces, pre, block = refs
    seq_len = pre.shape[0] // 2
    rows = block.shape[0] // len(blocks[0])
    if not has_prev:
        pieces[1:1] = [bp.at[pl.ds(2 * seq_len, rows), :]]
    for i, masks in enumerate(blocks):
        per = len(masks)
        fill_block(me, masks, pieces[i * per : (i + 1) * per], block)
        cols = ds(block_start(me, masks, rows), per * rows, per * rows)
        for s, x in ((0, bo), (1, bp)):
            own = pl.ds(s * seq_len, seq_len)
            part = dot(x[:seq_len, cols], block[...], 1, 0)
            if i > 0:
                part = part + pre[own, :]
            elif has_prev:
                part = part + prev[own, :]
            pre[own, :] = part


def gate(raw, scale):
    sig = pltpu.reciprocal(1.0 + jnp.exp2(raw * (-scale * LOG2E)), approx=True)
    out = raw * sig
    return out, sig + (out * scale if scale != 1.0 else out) * (1.0 - sig)


def forward_kernel(masks, bo, bp, prev, vgo, *refs):
    *pieces, act, slope, prob, dprob, mixed, block = refs
    me = lax.axis_index("dp")
    seq_len = vgo.shape[0]
    top = seq_len // 2
    far = pl.ds(seq_len, seq_len)
    fill_block(me, masks, pieces, block)
    rows = pieces[0].shape[0]
    cols = ds(block_start(me, masks, rows), len(masks) * rows, len(masks) * rows)
    for s, x in ((0, bo), (1, bp)):
        own = pl.ds(s * seq_len, seq_len)
        a, d = gate(prev[own, :] + dot(x[:seq_len, cols], block[...], 1, 0), 1.0)
        act[own, :] = a.astype(BF)
        slope[own, :] = d
    causal = lax.broadcasted_iota(jnp.int32, (top, top), 1) <= lax.broadcasted_iota(jnp.int32, (top, top), 0)
    none = jnp.zeros((top, top), BF)
    units = [(s, h) for s in range(2) for h in range(HL)]
    raws = []
    for s, h in units:
        own = pl.ds(s * seq_len, seq_len)
        raws.append(dot(act[own, pl.ds(h * DH, DH)], act[own, pl.ds(HALF + h * DH, DH)], 1, 1))
    probs = []
    for (s, h), raw in zip(units, raws):
        p0, d0 = gate(raw[:top, :top], SCALE)
        p1, d1 = gate(raw[top:, :], SCALE)
        p0, d0 = jnp.where(causal, p0, 0.0), jnp.where(causal, d0, 0.0)
        p2, d2 = jnp.where(causal, p1[:, top:], 0.0), jnp.where(causal, d1[:, top:], 0.0)
        whole = []
        for upper, left, right in ((p0, p1, p2), (d0, d1, d2)):
            whole.append(
                jnp.concatenate(
                    [
                        jnp.concatenate([upper.astype(BF), none], 1),
                        jnp.concatenate([left[:, :top].astype(BF), right.astype(BF)], 1),
                    ],
                    0,
                )
            )
        probs.append(whole[0])
        prob[s * HL + h] = whole[0]
        dprob[s * HL + h] = whole[1]
    for (s, h), p in zip(units, probs):
        at = pl.ds(h * DH, DH)
        val = bp[far, at] if s else vgo[:, at]
        mixed[pl.ds(s * seq_len, seq_len), pl.ds(h * DH, DH)] = dot(p, val, 1, 0)


def stats_kernel(length, mixed, vgo, bp, co, cp, prod, stats):
    seq_len = co.shape[0]
    prod[:seq_len, :] = vgo[:, HALF:].astype(F32) * co[...].astype(F32)
    prod[seq_len:, :] = bp[seq_len : 2 * seq_len, HALF:].astype(F32) * cp[...].astype(F32)
    lane = lax.broadcasted_iota(jnp.int32, (seq_len, 128), 1)
    row = lax.broadcasted_iota(jnp.int32, (seq_len, 128), 0)
    live = jnp.where(row < length[0, 0], 1.0, 0.0)
    for s in range(2):
        own = pl.ds(s * seq_len, seq_len)
        grad = prod[own, :]
        m = mixed[own, :]
        total = jnp.sum(m, axis=1, keepdims=True)
        off = m - total * (1.0 / HALF)
        cols = [
            total,
            jnp.sum(off * off, axis=1, keepdims=True),
            jnp.sum(grad, axis=1, keepdims=True),
            jnp.sum(grad * off, axis=1, keepdims=True),
        ]
        packed = live
        for i, col in enumerate(cols):
            packed = jnp.where(lane == i, col, packed)
        stats[:, own] = packed.T[:8, :]


def backward_kernel(far, xt, act, slope, prob, dprob, mixed, mine, theirs, vgo, bp, prod, co, cp, *refs):
    gpre, own_grads, far_grads, *terms = refs
    seq_len = co.shape[0]
    grad_refs = own_grads, far_grads
    units = []
    for s in range(2):
        own = pl.ds(s * seq_len, seq_len)
        other = pl.ds((1 - s) * seq_len, seq_len)
        a, b = mine[:, own], theirs[:, other]
        mean = (a[0:1] + b[0:1]) * (1.0 / F)
        mean_a, mean_b = a[0:1] * (1.0 / HALF), b[0:1] * (1.0 / HALF)
        gap = mean_a - mean_b
        variance = (a[1:2] + b[1:2] + gap * gap * (HALF * 0.5)) * (1.0 / F)
        live = (b if s else a)[4:5] > 0.5
        rate = jnp.where(live, SCALE * lax.rsqrt(variance * (SCALE * SCALE) + EPS), 0.0)
        c1 = (a[2:3] + b[2:3]) * (1.0 / F)
        cross = a[3:4] + b[3:4] + (mean_a - mean) * a[2:3] + (mean_b - mean) * b[2:3]
        c2 = cross * rate * (1.0 / F)
        cols = jnp.concatenate([mean, rate, c1, c2, mean, rate, c1, c2], 0).T
        mean, rate, c1, c2 = (cols[:, i : i + 1] for i in range(4))
        for h in range(HL):
            local = pl.ds(h * DH, DH)
            val, cot = (bp[pl.ds(seq_len, seq_len), local], cp[:, local]) if s else (vgo[:, local], co[:, local])
            normed = (mixed[own, local] - mean) * rate
            grad_refs[s][:, pl.ds(HALF + h * DH, DH)] = (normed * cot.astype(F32)).astype(BF)
            dmix = (rate * (prod[own, local] - c1 - normed * c2)).astype(BF)
            units.append((own, h, s * HL + h, val, dmix))
    dscores = [dot(dmix, val, 1, 1).astype(BF) * dprob[u] for _, _, u, val, dmix in units]
    for (own, h, u, _, dmix), dscore in zip(units, dscores):
        grad_refs[u // HL][:, pl.ds(h * DH, DH)] = dot(prob[u], dmix, 0, 0).astype(BF)
        q_at, k_at = pl.ds(h * DH, DH), pl.ds(HALF + h * DH, DH)
        dq = dot(dscore, act[own, k_at], 1, 0)
        dk = dot(dscore, act[own, q_at], 0, 0)
        gpre[own, q_at] = (dq * slope[own, q_at]).astype(BF)
        gpre[own, k_at] = (dk * slope[own, k_at]).astype(BF)
    rows = terms[0].shape[0]
    for m, term in zip(far, terms):
        term[...] = dot(xt[m * rows : (m + 1) * rows, :], gpre[...], 1, 0).astype(BF)


def term_kernel(near, xt, gpre, *terms):
    rows = terms[0].shape[0]
    for first in range(0, len(near), 2):
        m = near[first]
        both = dot(xt[m * rows : (m + 2) * rows, :], gpre[...], 1, 0).astype(BF)
        terms[first][...] = both[:rows, :]
        terms[first + 1][...] = both[rows:, :]


def fold_kernel(first, added, out):
    out[...] = (first[...].astype(F32) + added[...].astype(F32)).astype(BF)


def near_kernel(own, x, far, y, out_own, out_far):
    out_own[...] = own[...].astype(F32) + x[...].astype(F32)
    out_far[...] = far[...].astype(F32) + y[...].astype(F32)


def input_kernel(blocks, mine, bp, *refs):
    *pieces, gpre, own_out, other_out, block = refs
    me = lax.axis_index("dp")
    rows = mine.shape[0]
    seq_len = own_out.shape[0]
    pieces = [mine, bp.at[pl.ds(2 * seq_len, rows), :], *pieces]
    done = 0
    for masks in blocks:
        fill_block(me, masks, pieces[done : done + len(masks)], block)
        done += len(masks)
        cols = ds(block_start(me, masks, rows), len(masks) * rows, len(masks) * rows)
        for s, out in ((0, own_out), (1, other_out)):
            out[:, cols] = dot(gpre[pl.ds(s * seq_len, seq_len), :], block[...], 1, 1).astype(out.dtype)


def collect_kernel(gi_o, gi_r, own, far, gi, gv, gg):
    core = lax.rem(lax.axis_index("dp"), 2)
    gi[...] = (gi_o[...] + gi_r[...].astype(F32)).astype(BF)
    for c, ref in ((core, own), (1 - core, far)):
        for i, out in enumerate((gv, gg)):
            out[:, ds(c * HALF, HALF, HALF)] = ref[:, pl.ds(i * HALF, HALF)]


def weight_kernel(own, x, far, y, out):
    core = lax.rem(lax.axis_index("dp"), 2)
    for c, near, added in ((core, own, x), (1 - core, far, y)):
        for side in range(2):
            at = pl.ds(side * HALF, HALF)
            out[:, ds(side * F + c * HALF, HALF, HALF)] = near[:, at] + added[:, at].astype(F32)


def like(shape, kind):
    return jax.ShapeDtypeStruct(shape, kind)


def halve(terms, count):
    bit = count // 2
    while bit >= 8:
        terms = {
            m: (t.astype(F32) + pair(terms[m + bit], bit).astype(F32)).astype(BF) for m, t in terms.items() if m < bit
        }
        bit //= 2
    return terms


def on_device(inputs, values, gate_values, out_grad, lengths, qk_weight):
    count = lax.axis_size("dp")
    core = lax.rem(lax.axis_index("dp"), 2)
    xo, vo, go, grads = inputs[0, 0], values[0, 0], gate_values[0, 0], out_grad[0, 0]
    shard = qk_weight[0]
    rows, depth = shard.shape[0], xo.shape[1]
    seq_len = xo.shape[0]
    two = 2 * seq_len
    per = 256 // rows
    blocks = [tuple(range(b, b + per)) for b in range(0, count, per)]
    block = pltpu.VMEM((per * rows, F), BF)

    def half(x, c):
        return lax.dynamic_slice_in_dim(x, c * HALF, HALF, 1)

    def held(some):
        return [pieces[m] for masks in some for m in masks if m != 1]

    mine, other = (jnp.concatenate([half(shard[:, :F], c), half(shard[:, F:], c)], 1) for c in (core, 1 - core))
    bundle, vgo = call(
        pack_kernel, 0.001, [like((two + rows, F), BF), like((seq_len, F), BF)], other, xo, vo, go
    )
    pieces = {0: mine}
    pieces[2] = pair(mine, 2)
    pieces[5] = pair(other, 5)
    partner = pair(after(bundle, mine), 1)
    cp = from_next(half(after(grads, partner), 1 - core), 1)
    co = from_next(half(after(grads, partner), core))
    pieces[3] = pair(after(other, partner), 3)
    pieces[4] = pair(after(mine, partner), 4)
    xt = call(
        functools.partial(turn_kernel, count),
        10,
        like((depth, two), BF),
        bundle,
        partner,
        scratch=[pltpu.VMEM((depth, two), BF)],
    )
    pieces[6] = pair(pieces[2], 4)
    pieces[7] = pair(pieces[5], 2)
    pieces[1] = partner[two:]
    bit = 8
    while bit < count:
        for m in range(bit):
            pieces[m + bit] = pair(pieces[m], bit)
        bit *= 2
    first = functools.partial(pre_kernel, blocks[:1], False)
    pre = call(first, 0.001, like((two, F), F32), bundle, partner, *held(blocks[:1]), scratch=[block])
    more = functools.partial(pre_kernel, blocks[1:-1], True)
    pre = call(more, 0.001, like((two, F), F32), bundle, partner, pre, *held(blocks[1:-1]), scratch=[block])
    co, pre = lax.optimization_barrier((co, pre))
    act, slope, prob, dprob, mixed = call(
        functools.partial(forward_kernel, blocks[-1]),
        0.001,
        [
            like((two, F), BF),
            like((two, F), F32),
            like((2 * HL, seq_len, seq_len), BF),
            like((2 * HL, seq_len, seq_len), BF),
            like((two, HALF), F32),
        ],
        bundle,
        partner,
        pre,
        vgo,
        *held(blocks[-1:]),
        scratch=[block],
    )
    prod, stats = call(
        stats_kernel,
        1, [like((two, HALF), F32), like((8, two), F32)], lengths, mixed, vgo, partner, co, cp
    )
    theirs = pair(stats, 1)

    far = [m for m in range(count) if m % 8 >= 6]
    near = [m for m in range(count) if m % 8 < 6]
    gpre, own_g, far_g, *terms = call(
        functools.partial(backward_kernel, far),
        0.1,
        [like((two, F), BF)] + [like((seq_len, F), BF)] * 2 + [like((rows, F), BF)] * len(far),
        xt,
        act,
        slope,
        prob,
        dprob,
        mixed,
        stats,
        theirs,
        vgo,
        partner,
        prod,
        co,
        cp,
    )
    diagonal = halve(dict(zip(far, terms)), count)
    far_g = pair(far_g, 1)
    by_x, by_y = lax.optimization_barrier((pair(diagonal[6], 2), pair(diagonal[7], 4)))
    terms = call(functools.partial(term_kernel, near), 1, [like((rows, F), BF)] * len(near), xt, gpre)
    t = halve(dict(zip(near, terms)), count)
    x_r, y_r = lax.optimization_barrier((pair(t[2], 2), pair(t[5], 5)))
    far_t = pair(after(t[1], far_g), 1)
    near_own, near_far = call(near_kernel, 0.001, [like((rows, F), F32)] * 2, t[0], x_r, far_t, y_r)
    gi_o, gi_other = call(
        functools.partial(input_kernel, blocks),
        10,
        [like((seq_len, depth), F32), like((seq_len, depth), BF)],
        mine,
        partner,
        *held(blocks)[1:],
        gpre,
        scratch=[block],
    )
    gi_r = pair(after(gi_other, far_t), 1)
    send_y = call(fold_kernel, 0.3, like((rows, F), BF), t[4], by_x)
    send_x = call(fold_kernel, 0.3, like((rows, F), BF), t[3], by_y)
    grad_in, grad_val, grad_gate = call(
        collect_kernel, 0.3, [like((seq_len, F), BF)] * 3, gi_o, gi_r, own_g, far_g
    )
    sums = [near_own, pair(send_y, 4), near_far, pair(send_x, 3)]
    sums, _ = lax.optimization_barrier((sums, (grad_in, grad_val, grad_gate)))
    grad_shard = call(weight_kernel, 1, like((rows, 2 * F), F32), *sums)
    return (grad_in[None, None], grad_val[None, None], grad_gate[None, None], grad_shard[None])


def solution(mesh):
    return jax.shard_map(
        on_device,
        mesh=mesh,
        in_specs=(
            P("segment", "dp", None, None),
            P("segment", "dp", None, None),
            P("segment", "dp", None, None),
            P("segment", "dp", None, None),
            P("segment", "dp"),
            P("segment", "dp", None),
        ),
        out_specs=(
            P("segment", "dp", None, None),
            P("segment", "dp", None, None),
            P("segment", "dp", None, None),
            P("segment", "dp", None),
        ),
        check_vma=False,
    )
```

```python
import functools

import jax
import jax.numpy as jnp
from jax import lax
from jax.experimental import pallas as pl
from jax.experimental.pallas import tpu as pltpu
from jax.sharding import PartitionSpec as P

H = 8
DH = 128
F = H * DH
HALF = F // 2
HL = H // 2
SCALE = DH**-0.5
EPS = 1e-05
LOG2E = 1.4426950408889634
BF = jnp.bfloat16
F32 = jnp.float32
UNIT = 1e9
PARTS = 4

VMEM = pl.BlockSpec(memory_space=pltpu.VMEM)
SMEM = pl.BlockSpec(memory_space=pltpu.SMEM)


def pair(x, mask):
    count = lax.axis_size("dp")
    return lax.ppermute(x, "dp", [(i, i ^ mask) for i in range(count)])


def from_next(x, mask=0):
    dp, seg = lax.axis_size("dp"), lax.axis_size("segment")
    return lax.ppermute(
        x,
        ("dp", "segment"),
        [(i * seg + s, (i ^ mask) * seg + (s - 1) % seg) for i in range(dp) for s in range(seg)],
    )


def call(body, cost, out_shape, *args, scratch=()):
    return pl.pallas_call(
        body,
        out_shape=out_shape,
        in_specs=[SMEM if x.dtype == jnp.int32 else VMEM for x in args],
        out_specs=jax.tree.map(lambda _: VMEM, out_shape),
        scratch_shapes=list(scratch),
        cost_estimate=pl.CostEstimate(flops=int(cost * UNIT), bytes_accessed=int(cost * UNIT), transcendentals=0),
        compiler_params=pltpu.CompilerParams(vmem_limit_bytes=20 << 20),
    )(*args)


def dot(a, b, ca, cb):
    return lax.dot_general(a, b, (((ca,), (cb,)), ((), ())), preferred_element_type=F32)


def ds(start, size, align):
    return pl.ds(pl.multiple_of(start, align), size)


def after(x, *deps):
    return lax.optimization_barrier((x, *deps))[0]


def block_start(me, masks, rows):
    return lax.div(lax.bitwise_xor(me, masks[0]), len(masks)) * (len(masks) * rows)


def fill_block(me, masks, piece_refs, block):
    rows = piece_refs[0].shape[0]
    for m, ref in zip(masks, piece_refs):
        at = lax.rem(lax.bitwise_xor(me, m), len(masks)) * rows
        block[ds(at, rows, rows), :] = ref[...]


def pack_kernel(other, x, values, gates, bundle, vg):
    core = lax.rem(lax.axis_index("dp"), 2)
    seq_len, rows = x.shape[0], other.shape[0]
    bundle[:seq_len, :] = x[...]
    bundle[pl.ds(2 * seq_len, rows), :] = other[...]
    for i, ref in enumerate((values, gates)):
        at = pl.ds(i * HALF, HALF)
        vg[:, at] = ref[:, ds(core * HALF, HALF, HALF)]
        bundle[pl.ds(seq_len, seq_len), at] = ref[:, ds((1 - core) * HALF, HALF, HALF)]


def turn_kernel(count, bo, bp, xt, natural):
    depth, seq_len = xt.shape[0], xt.shape[1] // 2
    rows = depth // count
    natural[:, :seq_len] = bo[:seq_len, :].T
    natural[:, seq_len:] = bp[:seq_len, :].T
    for m in range(count):
        xt[m * rows : (m + 1) * rows, :] = natural[ds(lax.bitwise_xor(lax.axis_index("dp"), m) * rows, rows, rows), :]


def pre_kernel(blocks, has_prev, bo, bp, *refs):
    me = lax.axis_index("dp")
    if has_prev:
        prev, refs = refs[0], refs[1:]
    *pieces, pre, block = refs
    seq_len = pre.shape[0] // 2
    rows = block.shape[0] // len(blocks[0])
    if not has_prev:
        pieces[1:1] = [bp.at[pl.ds(2 * seq_len, rows), :]]
    for i, masks in enumerate(blocks):
        per = len(masks)
        fill_block(me, masks, pieces[i * per : (i + 1) * per], block)
        cols = ds(block_start(me, masks, rows), per * rows, per * rows)
        for s, x in ((0, bo), (1, bp)):
            own = pl.ds(s * seq_len, seq_len)
            part = dot(x[:seq_len, cols], block[...], 1, 0)
            if i > 0:
                part = part + pre[own, :]
            elif has_prev:
                part = part + prev[own, :]
            pre[own, :] = part


def sigmoid(raw, scale):
    return pltpu.reciprocal(1.0 + jnp.exp2(raw * (-scale * LOG2E)), approx=True)


def lower_half(upper, lower, causal):
    top = causal.shape[0]
    upper = jnp.where(causal, upper, 0.0).astype(BF)
    right = jnp.where(causal, lower[:, top:], 0.0).astype(BF)
    return jnp.concatenate(
        [
            jnp.concatenate([upper, jnp.zeros((top, top), BF)], 1),
            jnp.concatenate([lower[:, :top].astype(BF), right], 1),
        ],
        0,
    )


def slope_kernel(act, sig, slope):
    s = sig[...]
    slope[...] = s + act[...].astype(F32) * (1.0 - s)


def forward_kernel(masks, bo, bp, prev, vgo, *refs):
    *pieces, act, sigs, prob, dprob, mixed, block = refs
    me = lax.axis_index("dp")
    seq_len = vgo.shape[0]
    top = seq_len // 2
    far = pl.ds(seq_len, seq_len)
    fill_block(me, masks, pieces, block)
    rows = pieces[0].shape[0]
    cols = ds(block_start(me, masks, rows), len(masks) * rows, len(masks) * rows)
    for s, x in ((0, bo), (1, bp)):
        own = pl.ds(s * seq_len, seq_len)
        v = prev[own, :] + dot(x[:seq_len, cols], block[...], 1, 0)
        sig = sigmoid(v, 1.0)
        sigs[own, :] = sig
        act[own, :] = (v * sig).astype(BF)
    causal = lax.broadcasted_iota(jnp.int32, (top, top), 1) <= lax.broadcasted_iota(jnp.int32, (top, top), 0)
    units = [(s, h) for s in range(2) for h in range(HL)]
    raws = []
    for s, h in units:
        own = pl.ds(s * seq_len, seq_len)
        raws.append(dot(act[own, pl.ds(h * DH, DH)], act[own, pl.ds(HALF + h * DH, DH)], 1, 1))
    probs = []
    for (s, h), raw in zip(units, raws):
        halves = raw[:top, :top], raw[top:, :]
        sigs_h = [sigmoid(x, SCALE) for x in halves]
        outs = [x * sig for x, sig in zip(halves, sigs_h)]
        p = lower_half(*outs, causal)
        probs.append(p)
        prob[s * HL + h] = p
        dprob[s * HL + h] = lower_half(*(sig + o * SCALE * (1.0 - sig) for o, sig in zip(outs, sigs_h)), causal)
    for (s, h), p in zip(units, probs):
        at = pl.ds(h * DH, DH)
        val = bp[far, at] if s else vgo[:, at]
        mixed[pl.ds(s * seq_len, seq_len), pl.ds(h * DH, DH)] = dot(p, val, 1, 0)


def stats_kernel(length, mixed, vgo, bp, co, cp, prod, stats):
    seq_len = co.shape[0]
    prod[:seq_len, :] = vgo[:, HALF:].astype(F32) * co[...].astype(F32)
    prod[seq_len:, :] = bp[seq_len : 2 * seq_len, HALF:].astype(F32) * cp[...].astype(F32)
    lane = lax.broadcasted_iota(jnp.int32, (seq_len, 128), 1)
    row = lax.broadcasted_iota(jnp.int32, (seq_len, 128), 0)
    live = jnp.where(row < length[0, 0], 1.0, 0.0)
    for s in range(2):
        own = pl.ds(s * seq_len, seq_len)
        grad = prod[own, :]
        m = mixed[own, :]
        total = jnp.sum(m, axis=1, keepdims=True)
        off = m - total * (1.0 / HALF)
        cols = [
            total,
            jnp.sum(off * off, axis=1, keepdims=True),
            jnp.sum(grad, axis=1, keepdims=True),
            jnp.sum(grad * off, axis=1, keepdims=True),
        ]
        packed = live
        for i, col in enumerate(cols):
            packed = jnp.where(lane == i, col, packed)
        stats[:, own] = packed.T[:8, :]


def row_factors(mine, theirs, s):
    seq_len = mine.shape[1] // 2
    a, b = mine[:, pl.ds(s * seq_len, seq_len)], theirs[:, pl.ds((1 - s) * seq_len, seq_len)]
    mean = (a[0:1] + b[0:1]) * (1.0 / F)
    mean_a, mean_b = a[0:1] * (1.0 / HALF), b[0:1] * (1.0 / HALF)
    gap = mean_a - mean_b
    variance = (a[1:2] + b[1:2] + gap * gap * (HALF * 0.5)) * (1.0 / F)
    live = (b if s else a)[4:5] > 0.5
    rate = jnp.where(live, SCALE * lax.rsqrt(variance * (SCALE * SCALE) + EPS), 0.0)
    c1 = (a[2:3] + b[2:3]) * (1.0 / F)
    cross = a[3:4] + b[3:4] + (mean_a - mean) * a[2:3] + (mean_b - mean) * b[2:3]
    c2 = cross * rate * (1.0 / F)
    cols = jnp.concatenate([mean, rate, c1, c2, mean, rate, c1, c2], 0).T
    return [cols[:, i : i + 1] for i in range(4)]


def backward_kernel(far, xt, act, slope, prob_slope, mixed, mine, theirs, vgo, bp, prod, *refs):
    gpre, dmixed, *terms = refs
    seq_len = vgo.shape[0]
    units = []
    for s in range(2):
        own = pl.ds(s * seq_len, seq_len)
        mean, rate, c1, c2 = row_factors(mine, theirs, s)
        for h in range(HL):
            local = pl.ds(h * DH, DH)
            val = bp[pl.ds(seq_len, seq_len), local] if s else vgo[:, local]
            normed = (mixed[own, local] - mean) * rate
            dmix = (rate * (prod[own, local] - c1 - normed * c2)).astype(BF)
            dmixed[own, local] = dmix
            units.append((own, h, s * HL + h, val, dmix))
    dscores = [dot(dmix, val, 1, 1).astype(BF) * prob_slope[u] for _, _, u, val, dmix in units]
    for (own, h, _, _, _), dscore in zip(units, dscores):
        q_at, k_at = pl.ds(h * DH, DH), pl.ds(HALF + h * DH, DH)
        dq = dot(dscore, act[own, k_at], 1, 0)
        dk = dot(dscore, act[own, q_at], 0, 0)
        gpre[own, q_at] = (dq * slope[own, q_at]).astype(BF)
        gpre[own, k_at] = (dk * slope[own, k_at]).astype(BF)
    rows = terms[0].shape[0]
    for m, term in zip(far, terms):
        term[...] = dot(xt[m * rows : (m + 1) * rows, :], gpre[...], 1, 0).astype(BF)


def grad_kernel(prob, dmixed, mixed, mine, theirs, co, cp, own_grads, far_grads):
    seq_len = co.shape[0]
    for s, (cot, out) in enumerate(((co, own_grads), (cp, far_grads))):
        own = pl.ds(s * seq_len, seq_len)
        mean, rate, _, _ = row_factors(mine, theirs, s)
        out[:, HALF:] = ((mixed[own, :] - mean) * rate * cot[...].astype(F32)).astype(BF)
        for h in range(HL):
            at = pl.ds(h * DH, DH)
            out[:, at] = dot(prob[s * HL + h], dmixed[own, at], 0, 0).astype(BF)


def term_kernel(near, xt, gpre, *terms):
    rows = terms[0].shape[0]
    for first in range(0, len(near), 2):
        m = near[first]
        both = dot(xt[m * rows : (m + 2) * rows, :], gpre[...], 1, 0).astype(BF)
        terms[first][...] = both[:rows, :]
        terms[first + 1][...] = both[rows:, :]


def fold_kernel(first, added, out):
    out[...] = (first[...].astype(F32) + added[...].astype(F32)).astype(BF)


def near_kernel(own, x, far, y, out_own, out_far):
    out_own[...] = own[...].astype(F32) + x[...].astype(F32)
    out_far[...] = far[...].astype(F32) + y[...].astype(F32)


def input_kernel(blocks, mine, bp, *refs):
    *pieces, gpre, own_out, other_out, block = refs
    me = lax.axis_index("dp")
    rows = mine.shape[0]
    seq_len = own_out.shape[0]
    pieces = [mine, bp.at[pl.ds(2 * seq_len, rows), :], *pieces]
    done = 0
    for masks in blocks:
        fill_block(me, masks, pieces[done : done + len(masks)], block)
        done += len(masks)
        cols = ds(block_start(me, masks, rows), len(masks) * rows, len(masks) * rows)
        for s, out in ((0, own_out), (1, other_out)):
            out[:, cols] = dot(gpre[pl.ds(s * seq_len, seq_len), :], block[...], 1, 1).astype(out.dtype)


def collect_kernel(gi_o, gi_r, own, far, gi, gv, gg):
    core = lax.rem(lax.axis_index("dp"), 2)
    gi[...] = (gi_o[...] + gi_r[...].astype(F32)).astype(BF)
    for c, ref in ((core, own), (1 - core, far)):
        for i, out in enumerate((gv, gg)):
            out[:, ds(c * HALF, HALF, HALF)] = ref[:, pl.ds(i * HALF, HALF)]


def weight_kernel(own, x, far, y, out, whole, sems):
    core = lax.rem(lax.axis_index("dp"), 2)
    rows = own.shape[0] // PARTS
    copies = []
    for i in range(PARTS):
        block = pl.ds(i * rows, rows)
        for c, near, added in ((core, own, x), (1 - core, far, y)):
            for side in range(2):
                at = pl.ds(side * HALF, HALF)
                whole[block, ds(side * F + c * HALF, HALF, HALF)] = near[block, at] + added[block, at].astype(F32)
        copies.append(pltpu.make_async_copy(whole.at[block, :], out.at[block, :], sems.at[i]))
        copies[-1].start()
    for copy in copies:
        copy.wait()


def like(shape, kind):
    return jax.ShapeDtypeStruct(shape, kind)


def halve(terms, count):
    bit = count // 2
    while bit >= 8:
        terms = {
            m: (t.astype(F32) + pair(terms[m + bit], bit).astype(F32)).astype(BF) for m, t in terms.items() if m < bit
        }
        bit //= 2
    return terms


def on_device(inputs, values, gate_values, out_grad, lengths, qk_weight):
    count = lax.axis_size("dp")
    core = lax.rem(lax.axis_index("dp"), 2)
    xo, vo, go, grads = inputs[0, 0], values[0, 0], gate_values[0, 0], out_grad[0, 0]
    shard = qk_weight[0]
    rows, depth = shard.shape[0], xo.shape[1]
    seq_len = xo.shape[0]
    two = 2 * seq_len
    per = 256 // rows
    blocks = [tuple(range(b, b + per)) for b in range(0, count, per)]
    block = pltpu.VMEM((per * rows, F), BF)

    def half(x, c):
        return lax.dynamic_slice_in_dim(x, c * HALF, HALF, 1)

    def held(some):
        return [pieces[m] for masks in some for m in masks if m != 1]

    mine, other = (jnp.concatenate([half(shard[:, :F], c), half(shard[:, F:], c)], 1) for c in (core, 1 - core))
    bundle, vgo = call(
        pack_kernel, 0.001, [like((two + rows, F), BF), like((seq_len, F), BF)], other, xo, vo, go
    )
    pieces = {0: mine}
    pieces[2] = pair(mine, 2)
    pieces[5] = pair(other, 5)
    partner = pair(after(bundle, mine), 1)
    cp = from_next(half(after(grads, partner), 1 - core), 1)
    co = from_next(half(after(grads, partner), core))
    pieces[3] = pair(after(other, partner), 3)
    pieces[4] = pair(after(mine, partner), 4)
    xt = call(
        functools.partial(turn_kernel, count),
        1,
        like((depth, two), BF),
        bundle,
        partner,
        scratch=[pltpu.VMEM((depth, two), BF)],
    )
    pieces[6] = pair(pieces[2], 4)
    pieces[7] = pair(pieces[5], 2)
    pieces[1] = partner[two:]
    bit = 8
    while bit < count:
        for m in range(bit):
            pieces[m + bit] = pair(pieces[m], bit)
        bit *= 2
    first = functools.partial(pre_kernel, blocks[:1], False)
    pre = call(first, 0.001, like((two, F), F32), bundle, partner, *held(blocks[:1]), scratch=[block])
    more = functools.partial(pre_kernel, blocks[1:-1], True)
    pre = call(more, 0.001, like((two, F), F32), bundle, partner, after(pre, xt), *held(blocks[1:-1]), scratch=[block])
    co, pre = lax.optimization_barrier((co, pre))
    act, sigs, prob, prob_slope, mixed = call(
        functools.partial(forward_kernel, blocks[-1]),
        0.001,
        [
            like((two, F), BF),
            like((two, F), F32),
            like((2 * HL, seq_len, seq_len), BF),
            like((2 * HL, seq_len, seq_len), BF),
            like((two, HALF), F32),
        ],
        bundle,
        partner,
        pre,
        vgo,
        *held(blocks[-1:]),
        scratch=[block],
    )
    prod, stats = call(
        stats_kernel,
        1, [like((two, HALF), F32), like((8, two), F32)], lengths, mixed, vgo, partner, co, cp
    )
    theirs = pair(stats, 1)
    slope = call(slope_kernel, 0.3, like((two, F), F32), act, after(sigs, stats))

    far = [m for m in range(count) if m % 8 >= 6]
    near = [m for m in range(count) if m % 8 < 6]
    gpre, dmixed, *terms = call(
        functools.partial(backward_kernel, far),
        0.1,
        [like((two, F), BF), like((two, HALF), BF)] + [like((rows, F), BF)] * len(far),
        xt,
        act,
        slope,
        prob_slope,
        mixed,
        stats,
        theirs,
        vgo,
        partner,
        prod,
    )
    diagonal = halve(dict(zip(far, terms)), count)
    by_x, by_y = lax.optimization_barrier((pair(diagonal[6], 2), pair(diagonal[7], 4)))
    terms = call(functools.partial(term_kernel, near), 10, [like((rows, F), BF)] * len(near), xt, gpre)
    t = halve(dict(zip(near, terms)), count)
    own_g, far_g = call(
        grad_kernel, 3, [like((seq_len, F), BF)] * 2, prob, dmixed, mixed, stats, theirs, co, cp
    )
    far_g = pair(far_g, 1)
    x_r, y_r = lax.optimization_barrier((pair(t[2], 2), pair(t[5], 5)))
    far_t = pair(after(t[1], far_g), 1)
    near_own, near_far = call(near_kernel, 3, [like((rows, F), F32)] * 2, t[0], x_r, far_t, y_r)
    gi_o, gi_other = call(
        functools.partial(input_kernel, blocks),
        10,
        [like((seq_len, depth), F32), like((seq_len, depth), BF)],
        mine,
        partner,
        *held(blocks)[1:],
        gpre,
        scratch=[block],
    )
    gi_r = pair(after(gi_other, far_t), 1)
    send_y = call(fold_kernel, 0.3, like((rows, F), BF), t[4], by_x)
    send_x = call(fold_kernel, 0.3, like((rows, F), BF), t[3], by_y)
    grad_in, grad_val, grad_gate = call(
        collect_kernel, 0.3, [like((seq_len, F), BF)] * 3, gi_o, gi_r, own_g, far_g
    )
    sums = [near_own, pair(send_y, 4), near_far, pair(send_x, 3)]
    sums, _ = lax.optimization_barrier((sums, (grad_in, grad_val, grad_gate)))
    grad_shard = pl.pallas_call(
        weight_kernel,
        out_shape=like((rows, 2 * F), F32),
        in_specs=[VMEM] * 4,
        out_specs=pl.BlockSpec(memory_space=pl.ANY),
        scratch_shapes=[pltpu.VMEM((rows, 2 * F), F32), pltpu.SemaphoreType.DMA((PARTS,))],
        compiler_params=pltpu.CompilerParams(vmem_limit_bytes=20 << 20),
    )(*sums)
    return (grad_in[None, None], grad_val[None, None], grad_gate[None, None], grad_shard[None])


def solution(mesh):
    return jax.shard_map(
        on_device,
        mesh=mesh,
        in_specs=(
            P("segment", "dp", None, None),
            P("segment", "dp", None, None),
            P("segment", "dp", None, None),
            P("segment", "dp", None, None),
            P("segment", "dp"),
            P("segment", "dp", None),
        ),
        out_specs=(
            P("segment", "dp", None, None),
            P("segment", "dp", None, None),
            P("segment", "dp", None, None),
            P("segment", "dp", None),
        ),
        check_vma=False,
    )
```

```python
import functools

import jax
import jax.numpy as jnp
from jax import lax
from jax.experimental import pallas as pl
from jax.experimental.pallas import tpu as pltpu
from jax.sharding import PartitionSpec as P

H = 8
DH = 128
F = H * DH
HALF = F // 2
HL = H // 2
SCALE = DH**-0.5
EPS = 1e-05
LOG2E = 1.4426950408889634
BF = jnp.bfloat16
F32 = jnp.float32
UNIT = 1e9
PARTS = 4

VMEM = pl.BlockSpec(memory_space=pltpu.VMEM)
SMEM = pl.BlockSpec(memory_space=pltpu.SMEM)


def pair(x, mask):
    count = lax.axis_size("dp")
    return lax.ppermute(x, "dp", [(i, i ^ mask) for i in range(count)])


def from_next(x, mask=0):
    dp, seg = lax.axis_size("dp"), lax.axis_size("segment")
    return lax.ppermute(
        x,
        ("dp", "segment"),
        [(i * seg + s, (i ^ mask) * seg + (s - 1) % seg) for i in range(dp) for s in range(seg)],
    )


def call(body, cost, out_shape, *args, scratch=()):
    return pl.pallas_call(
        body,
        out_shape=out_shape,
        in_specs=[SMEM if x.dtype == jnp.int32 else VMEM for x in args],
        out_specs=jax.tree.map(lambda _: VMEM, out_shape),
        scratch_shapes=list(scratch),
        cost_estimate=pl.CostEstimate(flops=int(cost * UNIT), bytes_accessed=int(cost * UNIT), transcendentals=0),
        compiler_params=pltpu.CompilerParams(vmem_limit_bytes=20 << 20),
    )(*args)


def dot(a, b, ca, cb):
    return lax.dot_general(a, b, (((ca,), (cb,)), ((), ())), preferred_element_type=F32)


def ds(start, size, align):
    return pl.ds(pl.multiple_of(start, align), size)


def after(x, *deps):
    return lax.optimization_barrier((x, *deps))[0]


def block_start(me, masks, rows):
    return lax.div(lax.bitwise_xor(me, masks[0]), len(masks)) * (len(masks) * rows)


def fill_block(me, masks, piece_refs, block):
    rows = piece_refs[0].shape[0]
    for m, ref in zip(masks, piece_refs):
        at = lax.rem(lax.bitwise_xor(me, m), len(masks)) * rows
        block[ds(at, rows, rows), :] = ref[...]


def pack_kernel(other, x, values, gates, bundle, vg):
    core = lax.rem(lax.axis_index("dp"), 2)
    seq_len, rows = x.shape[0], other.shape[0]
    bundle[:seq_len, :] = x[...]
    bundle[pl.ds(2 * seq_len, rows), :] = other[...]
    for i, ref in enumerate((values, gates)):
        at = pl.ds(i * HALF, HALF)
        vg[:, at] = ref[:, ds(core * HALF, HALF, HALF)]
        bundle[pl.ds(seq_len, seq_len), at] = ref[:, ds((1 - core) * HALF, HALF, HALF)]


def turn_kernel(count, bo, bp, xt, natural):
    depth, seq_len = xt.shape[0], xt.shape[1] // 2
    rows = depth // count
    natural[:, :seq_len] = bo[:seq_len, :].T
    natural[:, seq_len:] = bp[:seq_len, :].T
    for m in range(count):
        xt[m * rows : (m + 1) * rows, :] = natural[ds(lax.bitwise_xor(lax.axis_index("dp"), m) * rows, rows, rows), :]


def pre_kernel(blocks, has_prev, bo, bp, *refs):
    me = lax.axis_index("dp")
    if has_prev:
        prev, refs = refs[0], refs[1:]
    *pieces, pre, block = refs
    seq_len = pre.shape[0] // 2
    rows = block.shape[0] // len(blocks[0])
    if not has_prev:
        pieces[1:1] = [bp.at[pl.ds(2 * seq_len, rows), :]]
    for i, masks in enumerate(blocks):
        per = len(masks)
        fill_block(me, masks, pieces[i * per : (i + 1) * per], block)
        cols = ds(block_start(me, masks, rows), per * rows, per * rows)
        for s, x in ((0, bo), (1, bp)):
            own = pl.ds(s * seq_len, seq_len)
            part = dot(x[:seq_len, cols], block[...], 1, 0)
            if i > 0:
                part = part + pre[own, :]
            elif has_prev:
                part = part + prev[own, :]
            pre[own, :] = part


def sigmoid(raw, scale):
    return pltpu.reciprocal(1.0 + jnp.exp2(raw * (-scale * LOG2E)), approx=True)


def lower_half(upper, lower, causal):
    top = causal.shape[0]
    upper = jnp.where(causal, upper, 0.0).astype(BF)
    right = jnp.where(causal, lower[:, top:], 0.0).astype(BF)
    return jnp.concatenate(
        [
            jnp.concatenate([upper, jnp.zeros((top, top), BF)], 1),
            jnp.concatenate([lower[:, :top].astype(BF), right], 1),
        ],
        0,
    )


def slope_kernel(act, sig, slope):
    s = sig[...]
    slope[...] = s + act[...].astype(F32) * (1.0 - s)


def forward_kernel(masks, bo, bp, prev, vgo, *refs):
    *pieces, act, sigs, prob, dprob, mixed, block = refs
    me = lax.axis_index("dp")
    seq_len = vgo.shape[0]
    top = seq_len // 2
    far = pl.ds(seq_len, seq_len)
    fill_block(me, masks, pieces, block)
    rows = pieces[0].shape[0]
    cols = ds(block_start(me, masks, rows), len(masks) * rows, len(masks) * rows)
    for s, x in ((0, bo), (1, bp)):
        own = pl.ds(s * seq_len, seq_len)
        v = prev[own, :] + dot(x[:seq_len, cols], block[...], 1, 0)
        sig = sigmoid(v, 1.0)
        sigs[own, :] = sig
        act[own, :] = (v * sig).astype(BF)
    causal = lax.broadcasted_iota(jnp.int32, (top, top), 1) <= lax.broadcasted_iota(jnp.int32, (top, top), 0)
    units = [(s, h) for s in range(2) for h in range(HL)]
    raws = []
    for s, h in units:
        own = pl.ds(s * seq_len, seq_len)
        q, k = act[own, pl.ds(h * DH, DH)], act[own, pl.ds(HALF + h * DH, DH)]
        raws.append((dot(q[:top], k[:top], 1, 1), dot(q[top:], k, 1, 1)))
    probs = []
    for (s, h), raw in zip(units, raws):
        sigs_h = [sigmoid(x, SCALE) for x in raw]
        outs = [x * sig for x, sig in zip(raw, sigs_h)]
        p = lower_half(*outs, causal)
        probs.append(p)
        prob[s * HL + h] = p
        dprob[s * HL + h] = lower_half(*(sig + o * SCALE * (1.0 - sig) for o, sig in zip(outs, sigs_h)), causal)
    for (s, h), p in zip(units, probs):
        at = pl.ds(h * DH, DH)
        val = bp[far, at] if s else vgo[:, at]
        mixed[pl.ds(s * seq_len, top), at] = dot(p[:top, :top], val[:top], 1, 0)
        mixed[pl.ds(s * seq_len + top, top), at] = dot(p[top:], val, 1, 0)


def stats_kernel(length, mixed, vgo, bp, co, cp, prod, stats):
    seq_len = co.shape[0]
    prod[:seq_len, :] = vgo[:, HALF:].astype(F32) * co[...].astype(F32)
    prod[seq_len:, :] = bp[seq_len : 2 * seq_len, HALF:].astype(F32) * cp[...].astype(F32)
    lane = lax.broadcasted_iota(jnp.int32, (seq_len, 128), 1)
    row = lax.broadcasted_iota(jnp.int32, (seq_len, 128), 0)
    live = jnp.where(row < length[0, 0], 1.0, 0.0)
    for s in range(2):
        own = pl.ds(s * seq_len, seq_len)
        grad = prod[own, :]
        m = mixed[own, :]
        total = jnp.sum(m, axis=1, keepdims=True)
        off = m - total * (1.0 / HALF)
        cols = [
            total,
            jnp.sum(off * off, axis=1, keepdims=True),
            jnp.sum(grad, axis=1, keepdims=True),
            jnp.sum(grad * off, axis=1, keepdims=True),
        ]
        packed = live
        for i, col in enumerate(cols):
            packed = jnp.where(lane == i, col, packed)
        stats[:, own] = packed.T[:8, :]


def row_factors(mine, theirs, s):
    seq_len = mine.shape[1] // 2
    a, b = mine[:, pl.ds(s * seq_len, seq_len)], theirs[:, pl.ds((1 - s) * seq_len, seq_len)]
    mean = (a[0:1] + b[0:1]) * (1.0 / F)
    mean_a, mean_b = a[0:1] * (1.0 / HALF), b[0:1] * (1.0 / HALF)
    gap = mean_a - mean_b
    variance = (a[1:2] + b[1:2] + gap * gap * (HALF * 0.5)) * (1.0 / F)
    live = (b if s else a)[4:5] > 0.5
    rate = jnp.where(live, SCALE * lax.rsqrt(variance * (SCALE * SCALE) + EPS), 0.0)
    c1 = (a[2:3] + b[2:3]) * (1.0 / F)
    cross = a[3:4] + b[3:4] + (mean_a - mean) * a[2:3] + (mean_b - mean) * b[2:3]
    c2 = cross * rate * (1.0 / F)
    cols = jnp.concatenate([mean, rate, c1, c2, mean, rate, c1, c2], 0).T
    return [cols[:, i : i + 1] for i in range(4)]


def backward_kernel(far, xt, act, slope, prob_slope, mixed, mine, theirs, vgo, bp, prod, *refs):
    gpre, dmixed, *terms = refs
    seq_len = vgo.shape[0]
    units = []
    for s in range(2):
        own = pl.ds(s * seq_len, seq_len)
        mean, rate, c1, c2 = row_factors(mine, theirs, s)
        for h in range(HL):
            local = pl.ds(h * DH, DH)
            val = bp[pl.ds(seq_len, seq_len), local] if s else vgo[:, local]
            normed = (mixed[own, local] - mean) * rate
            dmix = (rate * (prod[own, local] - c1 - normed * c2)).astype(BF)
            dmixed[own, local] = dmix
            units.append((own, h, s * HL + h, val, dmix))
    dscores = []
    for _, _, u, val, dmix in units:
        top = seq_len // 2
        upper = dot(dmix[:top], val[:top], 1, 1).astype(BF) * prob_slope[u][:top, :top]
        lower = dot(dmix[top:], val, 1, 1).astype(BF) * prob_slope[u][top:]
        dscores.append(jnp.concatenate([jnp.concatenate([upper, jnp.zeros_like(upper)], 1), lower], 0))
    for (own, h, _, _, _), dscore in zip(units, dscores):
        q_at, k_at = pl.ds(h * DH, DH), pl.ds(HALF + h * DH, DH)
        gpre[own, q_at] = (dot(dscore, act[own, k_at], 1, 0) * slope[own, q_at]).astype(BF)
    for (own, h, _, _, _), dscore in zip(units, dscores):
        q_at, k_at = pl.ds(h * DH, DH), pl.ds(HALF + h * DH, DH)
        gpre[own, k_at] = (dot(dscore, act[own, q_at], 0, 0) * slope[own, k_at]).astype(BF)
    rows = terms[0].shape[0]
    for m, term in zip(far, terms):
        term[...] = dot(xt[m * rows : (m + 1) * rows, :], gpre[...], 1, 0).astype(BF)


def grad_kernel(prob, dmixed, mixed, mine, theirs, co, cp, own_grads, far_grads):
    seq_len = co.shape[0]
    for s, (cot, out) in enumerate(((co, own_grads), (cp, far_grads))):
        own = pl.ds(s * seq_len, seq_len)
        mean, rate, _, _ = row_factors(mine, theirs, s)
        out[:, HALF:] = ((mixed[own, :] - mean) * rate * cot[...].astype(F32)).astype(BF)
        for h in range(HL):
            at = pl.ds(h * DH, DH)
            out[:, at] = dot(prob[s * HL + h], dmixed[own, at], 0, 0).astype(BF)


def term_kernel(near, xt, gpre, *terms):
    rows = terms[0].shape[0]
    for first in range(0, len(near), 2):
        m = near[first]
        both = dot(xt[m * rows : (m + 2) * rows, :], gpre[...], 1, 0).astype(BF)
        terms[first][...] = both[:rows, :]
        terms[first + 1][...] = both[rows:, :]


def fold_kernel(first, added, out):
    out[...] = (first[...].astype(F32) + added[...].astype(F32)).astype(BF)


def near_kernel(own, x, far, y, out_own, out_far):
    out_own[...] = own[...].astype(F32) + x[...].astype(F32)
    out_far[...] = far[...].astype(F32) + y[...].astype(F32)


def input_kernel(blocks, mine, bp, *refs):
    *pieces, gpre, own_out, other_out, block = refs
    me = lax.axis_index("dp")
    rows = mine.shape[0]
    seq_len = own_out.shape[0]
    pieces = [mine, bp.at[pl.ds(2 * seq_len, rows), :], *pieces]
    done = 0
    for masks in blocks:
        fill_block(me, masks, pieces[done : done + len(masks)], block)
        done += len(masks)
        cols = ds(block_start(me, masks, rows), len(masks) * rows, len(masks) * rows)
        for s, out in ((0, own_out), (1, other_out)):
            out[:, cols] = dot(gpre[pl.ds(s * seq_len, seq_len), :], block[...], 1, 1).astype(out.dtype)


def collect_kernel(gi_o, gi_r, own, far, gi, gv, gg):
    core = lax.rem(lax.axis_index("dp"), 2)
    gi[...] = (gi_o[...] + gi_r[...].astype(F32)).astype(BF)
    for c, ref in ((core, own), (1 - core, far)):
        for i, out in enumerate((gv, gg)):
            out[:, ds(c * HALF, HALF, HALF)] = ref[:, pl.ds(i * HALF, HALF)]


def weight_kernel(own, x, far, y, out, whole, sems):
    core = lax.rem(lax.axis_index("dp"), 2)
    rows = own.shape[0] // PARTS
    copies = []
    for i in range(PARTS):
        block = pl.ds(i * rows, rows)
        for c, near, added in ((core, own, x), (1 - core, far, y)):
            for side in range(2):
                at = pl.ds(side * HALF, HALF)
                whole[block, ds(side * F + c * HALF, HALF, HALF)] = near[block, at] + added[block, at].astype(F32)
        copies.append(pltpu.make_async_copy(whole.at[block, :], out.at[block, :], sems.at[i]))
        copies[-1].start()
    for copy in copies:
        copy.wait()


def like(shape, kind):
    return jax.ShapeDtypeStruct(shape, kind)


def halve(terms, count):
    bit = count // 2
    while bit >= 8:
        terms = {
            m: (t.astype(F32) + pair(terms[m + bit], bit).astype(F32)).astype(BF) for m, t in terms.items() if m < bit
        }
        bit //= 2
    return terms


def on_device(inputs, values, gate_values, out_grad, lengths, qk_weight):
    count = lax.axis_size("dp")
    core = lax.rem(lax.axis_index("dp"), 2)
    xo, vo, go, grads = inputs[0, 0], values[0, 0], gate_values[0, 0], out_grad[0, 0]
    shard = qk_weight[0]
    rows, depth = shard.shape[0], xo.shape[1]
    seq_len = xo.shape[0]
    two = 2 * seq_len
    per = 256 // rows
    blocks = [tuple(range(b, b + per)) for b in range(0, count, per)]
    block = pltpu.VMEM((per * rows, F), BF)

    def half(x, c):
        return lax.dynamic_slice_in_dim(x, c * HALF, HALF, 1)

    def held(some):
        return [pieces[m] for masks in some for m in masks if m != 1]

    mine, other = (jnp.concatenate([half(shard[:, :F], c), half(shard[:, F:], c)], 1) for c in (core, 1 - core))
    bundle, vgo = call(
        pack_kernel, 0.001, [like((two + rows, F), BF), like((seq_len, F), BF)], other, xo, vo, go
    )
    pieces = {0: mine}
    pieces[2] = pair(mine, 2)
    pieces[5] = pair(other, 5)
    partner = pair(after(bundle, mine), 1)
    cp = from_next(half(after(grads, partner), 1 - core), 1)
    co = from_next(half(after(grads, partner), core))
    pieces[3] = pair(after(other, partner), 3)
    pieces[4] = pair(after(mine, partner), 4)
    xt = call(
        functools.partial(turn_kernel, count),
        1,
        like((depth, two), BF),
        bundle,
        partner,
        scratch=[pltpu.VMEM((depth, two), BF)],
    )
    pieces[6] = pair(pieces[2], 4)
    pieces[7] = pair(pieces[5], 2)
    pieces[1] = partner[two:]
    bit = 8
    while bit < count:
        for m in range(bit):
            pieces[m + bit] = pair(pieces[m], bit)
        bit *= 2
    first = functools.partial(pre_kernel, blocks[:1], False)
    pre = call(first, 0.001, like((two, F), F32), bundle, partner, *held(blocks[:1]), scratch=[block])
    more = functools.partial(pre_kernel, blocks[1:-1], True)
    pre = call(more, 0.001, like((two, F), F32), bundle, partner, after(pre, xt), *held(blocks[1:-1]), scratch=[block])
    co, pre = lax.optimization_barrier((co, pre))
    act, sigs, prob, prob_slope, mixed = call(
        functools.partial(forward_kernel, blocks[-1]),
        0.001,
        [
            like((two, F), BF),
            like((two, F), F32),
            like((2 * HL, seq_len, seq_len), BF),
            like((2 * HL, seq_len, seq_len), BF),
            like((two, HALF), F32),
        ],
        bundle,
        partner,
        pre,
        vgo,
        *held(blocks[-1:]),
        scratch=[block],
    )
    prod, stats = call(
        stats_kernel,
        1, [like((two, HALF), F32), like((8, two), F32)], lengths, mixed, vgo, partner, co, cp
    )
    theirs = pair(stats, 1)
    slope = call(slope_kernel, 0.3, like((two, F), F32), act, after(sigs, stats))

    far = [m for m in range(count) if m % 8 >= 6]
    near = [m for m in range(count) if m % 8 < 6]
    gpre, dmixed, *terms = call(
        functools.partial(backward_kernel, far),
        0.1,
        [like((two, F), BF), like((two, HALF), BF)] + [like((rows, F), BF)] * len(far),
        xt,
        act,
        slope,
        prob_slope,
        mixed,
        stats,
        theirs,
        vgo,
        partner,
        prod,
    )
    diagonal = halve(dict(zip(far, terms)), count)
    by_x, by_y = lax.optimization_barrier((pair(diagonal[6], 2), pair(diagonal[7], 4)))
    terms = call(functools.partial(term_kernel, near), 10, [like((rows, F), BF)] * len(near), xt, gpre)
    t = halve(dict(zip(near, terms)), count)
    own_g, far_g = call(
        grad_kernel, 3, [like((seq_len, F), BF)] * 2, prob, dmixed, mixed, stats, theirs, co, cp
    )
    far_g = pair(far_g, 1)
    x_r, y_r = lax.optimization_barrier((pair(t[2], 2), pair(t[5], 5)))
    far_t = pair(after(t[1], far_g), 1)
    near_own, near_far = call(near_kernel, 3, [like((rows, F), F32)] * 2, t[0], x_r, far_t, y_r)
    gi_o, gi_other = call(
        functools.partial(input_kernel, blocks),
        10,
        [like((seq_len, depth), F32), like((seq_len, depth), BF)],
        mine,
        partner,
        *held(blocks)[1:],
        gpre,
        scratch=[block],
    )
    gi_r = pair(after(gi_other, far_t), 1)
    send_y = call(fold_kernel, 0.3, like((rows, F), BF), t[4], by_x)
    send_x = call(fold_kernel, 0.3, like((rows, F), BF), t[3], by_y)
    grad_in, grad_val, grad_gate = call(
        collect_kernel, 0.3, [like((seq_len, F), BF)] * 3, gi_o, gi_r, own_g, far_g
    )
    sums = [near_own, pair(send_y, 4), near_far, pair(send_x, 3)]
    sums, _ = lax.optimization_barrier((sums, (grad_in, grad_val, grad_gate)))
    grad_shard = pl.pallas_call(
        weight_kernel,
        out_shape=like((rows, 2 * F), F32),
        in_specs=[VMEM] * 4,
        out_specs=pl.BlockSpec(memory_space=pl.ANY),
        scratch_shapes=[pltpu.VMEM((rows, 2 * F), F32), pltpu.SemaphoreType.DMA((PARTS,))],
        compiler_params=pltpu.CompilerParams(vmem_limit_bytes=20 << 20),
    )(*sums)
    return (grad_in[None, None], grad_val[None, None], grad_gate[None, None], grad_shard[None])


def solution(mesh):
    return jax.shard_map(
        on_device,
        mesh=mesh,
        in_specs=(
            P("segment", "dp", None, None),
            P("segment", "dp", None, None),
            P("segment", "dp", None, None),
            P("segment", "dp", None, None),
            P("segment", "dp"),
            P("segment", "dp", None),
        ),
        out_specs=(
            P("segment", "dp", None, None),
            P("segment", "dp", None, None),
            P("segment", "dp", None, None),
            P("segment", "dp", None),
        ),
        check_vma=False,
    )
```

```python
import functools

import jax
import jax.numpy as jnp
from jax import lax
from jax.experimental import pallas as pl
from jax.experimental.pallas import tpu as pltpu
from jax.sharding import PartitionSpec as P

H = 8
DH = 128
F = H * DH
HALF = F // 2
HL = H // 2
SCALE = DH**-0.5
EPS = 1e-05
LOG2E = 1.4426950408889634
BF = jnp.bfloat16
F32 = jnp.float32
UNIT = 1e9
PARTS = 4

VMEM = pl.BlockSpec(memory_space=pltpu.VMEM)
SMEM = pl.BlockSpec(memory_space=pltpu.SMEM)


def pair(x, mask):
    count = lax.axis_size("dp")
    return lax.ppermute(x, "dp", [(i, i ^ mask) for i in range(count)])


def from_next(x, mask=0):
    dp, seg = lax.axis_size("dp"), lax.axis_size("segment")
    return lax.ppermute(
        x,
        ("dp", "segment"),
        [(i * seg + s, (i ^ mask) * seg + (s - 1) % seg) for i in range(dp) for s in range(seg)],
    )


def call(body, cost, out_shape, *args, scratch=()):
    return pl.pallas_call(
        body,
        out_shape=out_shape,
        in_specs=[SMEM if x.dtype == jnp.int32 else VMEM for x in args],
        out_specs=jax.tree.map(lambda _: VMEM, out_shape),
        scratch_shapes=list(scratch),
        cost_estimate=pl.CostEstimate(flops=int(cost * UNIT), bytes_accessed=int(cost * UNIT), transcendentals=0),
        compiler_params=pltpu.CompilerParams(vmem_limit_bytes=20 << 20),
    )(*args)


def dot(a, b, ca, cb):
    return lax.dot_general(a, b, (((ca,), (cb,)), ((), ())), preferred_element_type=F32)


def ds(start, size, align):
    return pl.ds(pl.multiple_of(start, align), size)


def after(x, *deps):
    return lax.optimization_barrier((x, *deps))[0]


def block_start(me, masks, rows):
    return lax.div(lax.bitwise_xor(me, masks[0]), len(masks)) * (len(masks) * rows)


def fill_block(me, masks, piece_refs, block):
    rows = piece_refs[0].shape[0]
    for m, ref in zip(masks, piece_refs):
        at = lax.rem(lax.bitwise_xor(me, m), len(masks)) * rows
        block[ds(at, rows, rows), :] = ref[...]


def pack_kernel(other, x, values, gates, bundle, vg):
    core = lax.rem(lax.axis_index("dp"), 2)
    seq_len, rows = x.shape[0], other.shape[0]
    bundle[:seq_len, :] = x[...]
    bundle[pl.ds(2 * seq_len, rows), :] = other[...]
    for i, ref in enumerate((values, gates)):
        at = pl.ds(i * HALF, HALF)
        vg[:, at] = ref[:, ds(core * HALF, HALF, HALF)]
        bundle[pl.ds(seq_len, seq_len), at] = ref[:, ds((1 - core) * HALF, HALF, HALF)]


def turn_kernel(count, bo, bp, xt, natural):
    depth, seq_len = xt.shape[0], xt.shape[1] // 2
    rows = depth // count
    natural[:, :seq_len] = bo[:seq_len, :].T
    natural[:, seq_len:] = bp[:seq_len, :].T
    for m in range(count):
        xt[m * rows : (m + 1) * rows, :] = natural[ds(lax.bitwise_xor(lax.axis_index("dp"), m) * rows, rows, rows), :]


def pre_kernel(blocks, has_prev, bo, bp, *refs):
    me = lax.axis_index("dp")
    if has_prev:
        prev, refs = refs[0], refs[1:]
    *pieces, pre, block = refs
    seq_len = pre.shape[0] // 2
    rows = block.shape[0] // len(blocks[0])
    if not has_prev:
        pieces[1:1] = [bp.at[pl.ds(2 * seq_len, rows), :]]
    for i, masks in enumerate(blocks):
        per = len(masks)
        fill_block(me, masks, pieces[i * per : (i + 1) * per], block)
        cols = ds(block_start(me, masks, rows), per * rows, per * rows)
        for s, x in ((0, bo), (1, bp)):
            own = pl.ds(s * seq_len, seq_len)
            part = dot(x[:seq_len, cols], block[...], 1, 0)
            if i > 0:
                part = part + pre[own, :]
            elif has_prev:
                part = part + prev[own, :]
            pre[own, :] = part


def sigmoid(raw, scale):
    return pltpu.reciprocal(1.0 + jnp.exp2(raw * (-scale * LOG2E)), approx=True)


def lower_half(upper, lower, causal):
    top = causal.shape[0]
    upper = jnp.where(causal, upper, 0.0).astype(BF)
    right = jnp.where(causal, lower[:, top:], 0.0).astype(BF)
    return jnp.concatenate(
        [
            jnp.concatenate([upper, jnp.zeros((top, top), BF)], 1),
            jnp.concatenate([lower[:, :top].astype(BF), right], 1),
        ],
        0,
    )


def slope_kernel(act, sig, slope):
    s = sig[...]
    slope[...] = s + act[...].astype(F32) * (1.0 - s)


def forward_kernel(masks, bo, bp, prev, vgo, *refs):
    *pieces, act, sigs, prob, dprob, mixed, block = refs
    me = lax.axis_index("dp")
    seq_len = vgo.shape[0]
    top = seq_len // 2
    far = pl.ds(seq_len, seq_len)
    fill_block(me, masks, pieces, block)
    rows = pieces[0].shape[0]
    cols = ds(block_start(me, masks, rows), len(masks) * rows, len(masks) * rows)
    for s, x in ((0, bo), (1, bp)):
        own = pl.ds(s * seq_len, seq_len)
        v = prev[own, :] + dot(x[:seq_len, cols], block[...], 1, 0)
        sig = sigmoid(v, 1.0)
        sigs[own, :] = sig
        act[own, :] = (v * sig).astype(BF)
    causal = lax.broadcasted_iota(jnp.int32, (top, top), 1) <= lax.broadcasted_iota(jnp.int32, (top, top), 0)
    units = [(s, h) for s in range(2) for h in range(HL)]
    raws = []
    for s, h in units:
        own = pl.ds(s * seq_len, seq_len)
        q, k = act[own, pl.ds(h * DH, DH)], act[own, pl.ds(HALF + h * DH, DH)]
        raws.append((dot(q[:top], k[:top], 1, 1), dot(q[top:], k, 1, 1)))
    probs = []
    for (s, h), raw in zip(units, raws):
        sigs_h = [sigmoid(x, SCALE) for x in raw]
        outs = [x * sig for x, sig in zip(raw, sigs_h)]
        p = lower_half(*outs, causal)
        probs.append(p)
        prob[s * HL + h] = p
        dprob[s * HL + h] = lower_half(*(sig + o * SCALE * (1.0 - sig) for o, sig in zip(outs, sigs_h)), causal)
    for (s, h), p in zip(units, probs):
        at = pl.ds(h * DH, DH)
        val = bp[far, at] if s else vgo[:, at]
        mixed[pl.ds(s * seq_len, top), at] = dot(p[:top, :top], val[:top], 1, 0)
        mixed[pl.ds(s * seq_len + top, top), at] = dot(p[top:], val, 1, 0)


def stats_kernel(length, mixed, vgo, bp, co, cp, prod, stats):
    seq_len = co.shape[0]
    prod[:seq_len, :] = vgo[:, HALF:].astype(F32) * co[...].astype(F32)
    prod[seq_len:, :] = bp[seq_len : 2 * seq_len, HALF:].astype(F32) * cp[...].astype(F32)
    lane = lax.broadcasted_iota(jnp.int32, (seq_len, 128), 1)
    row = lax.broadcasted_iota(jnp.int32, (seq_len, 128), 0)
    live = jnp.where(row < length[0, 0], 1.0, 0.0)
    for s in range(2):
        own = pl.ds(s * seq_len, seq_len)
        grad = prod[own, :]
        m = mixed[own, :]
        total = jnp.sum(m, axis=1, keepdims=True)
        off = m - total * (1.0 / HALF)
        cols = [
            total,
            jnp.sum(off * off, axis=1, keepdims=True),
            jnp.sum(grad, axis=1, keepdims=True),
            jnp.sum(grad * off, axis=1, keepdims=True),
        ]
        packed = live
        for i, col in enumerate(cols):
            packed = jnp.where(lane == i, col, packed)
        stats[:, own] = packed.T[:8, :]


def row_factors(mine, theirs, s):
    seq_len = mine.shape[1] // 2
    a, b = mine[:, pl.ds(s * seq_len, seq_len)], theirs[:, pl.ds((1 - s) * seq_len, seq_len)]
    mean = (a[0:1] + b[0:1]) * (1.0 / F)
    mean_a, mean_b = a[0:1] * (1.0 / HALF), b[0:1] * (1.0 / HALF)
    gap = mean_a - mean_b
    variance = (a[1:2] + b[1:2] + gap * gap * (HALF * 0.5)) * (1.0 / F)
    live = (b if s else a)[4:5] > 0.5
    rate = jnp.where(live, SCALE * lax.rsqrt(variance * (SCALE * SCALE) + EPS), 0.0)
    c1 = (a[2:3] + b[2:3]) * (1.0 / F)
    cross = a[3:4] + b[3:4] + (mean_a - mean) * a[2:3] + (mean_b - mean) * b[2:3]
    c2 = cross * rate * (1.0 / F)
    cols = jnp.concatenate([mean, rate, c1, c2, mean, rate, c1, c2], 0).T
    return [cols[:, i : i + 1] for i in range(4)]


def backward_kernel(far, xt, act, slope, prob_slope, mixed, mine, theirs, vgo, bp, prod, *refs):
    gpre, dmixed, *terms = refs
    seq_len = vgo.shape[0]
    units = []
    for s in range(2):
        own = pl.ds(s * seq_len, seq_len)
        mean, rate, c1, c2 = row_factors(mine, theirs, s)
        for h in range(HL):
            local = pl.ds(h * DH, DH)
            val = bp[pl.ds(seq_len, seq_len), local] if s else vgo[:, local]
            normed = (mixed[own, local] - mean) * rate
            dmix = (rate * (prod[own, local] - c1 - normed * c2)).astype(BF)
            dmixed[own, local] = dmix
            units.append((own, h, s * HL + h, val, dmix))
    dscores = []
    for _, _, u, val, dmix in units:
        top = seq_len // 2
        upper = dot(dmix[:top], val[:top], 1, 1).astype(BF) * prob_slope[u][:top, :top]
        lower = dot(dmix[top:], val, 1, 1).astype(BF) * prob_slope[u][top:]
        dscores.append(jnp.concatenate([jnp.concatenate([upper, jnp.zeros_like(upper)], 1), lower], 0))
    for (own, h, _, _, _), dscore in zip(units, dscores):
        q_at, k_at = pl.ds(h * DH, DH), pl.ds(HALF + h * DH, DH)
        gpre[own, q_at] = (dot(dscore, act[own, k_at], 1, 0) * slope[own, q_at]).astype(BF)
    for (own, h, _, _, _), dscore in zip(units, dscores):
        q_at, k_at = pl.ds(h * DH, DH), pl.ds(HALF + h * DH, DH)
        gpre[own, k_at] = (dot(dscore, act[own, q_at], 0, 0) * slope[own, k_at]).astype(BF)
    rows = terms[0].shape[0]
    for m, term in zip(far, terms):
        term[...] = dot(xt[m * rows : (m + 1) * rows, :], gpre[...], 1, 0).astype(BF)


def grad_kernel(prob, dmixed, mixed, mine, theirs, co, cp, own_grads, far_grads):
    seq_len = co.shape[0]
    for s, (cot, out) in enumerate(((co, own_grads), (cp, far_grads))):
        own = pl.ds(s * seq_len, seq_len)
        mean, rate, _, _ = row_factors(mine, theirs, s)
        out[:, HALF:] = ((mixed[own, :] - mean) * rate * cot[...].astype(F32)).astype(BF)
        for h in range(HL):
            at = pl.ds(h * DH, DH)
            out[:, at] = dot(prob[s * HL + h], dmixed[own, at], 0, 0).astype(BF)


def term_kernel(near, xt, gpre, *terms):
    rows = terms[0].shape[0]
    for first in range(0, len(near), 2):
        m = near[first]
        both = dot(xt[m * rows : (m + 2) * rows, :], gpre[...], 1, 0).astype(BF)
        terms[first][...] = both[:rows, :]
        terms[first + 1][...] = both[rows:, :]


def fold_kernel(first, added, out):
    out[...] = (first[...].astype(F32) + added[...].astype(F32)).astype(BF)


def near_kernel(own, x, far, y, out_own, out_far):
    out_own[...] = own[...].astype(F32) + x[...].astype(F32)
    out_far[...] = far[...].astype(F32) + y[...].astype(F32)


def input_kernel(blocks, mine, bp, *refs):
    *pieces, gpre, own_out, other_out, block = refs
    me = lax.axis_index("dp")
    rows = mine.shape[0]
    seq_len = own_out.shape[0]
    pieces = [mine, bp.at[pl.ds(2 * seq_len, rows), :], *pieces]
    done = 0
    for masks in blocks:
        fill_block(me, masks, pieces[done : done + len(masks)], block)
        done += len(masks)
        cols = ds(block_start(me, masks, rows), len(masks) * rows, len(masks) * rows)
        for s, out in ((0, own_out), (1, other_out)):
            out[:, cols] = dot(gpre[pl.ds(s * seq_len, seq_len), :], block[...], 1, 1).astype(out.dtype)


def collect_kernel(gi_o, gi_r, own, far, gi, gv, gg):
    core = lax.rem(lax.axis_index("dp"), 2)
    gi[...] = (gi_o[...] + gi_r[...].astype(F32)).astype(BF)
    for c, ref in ((core, own), (1 - core, far)):
        for i, out in enumerate((gv, gg)):
            out[:, ds(c * HALF, HALF, HALF)] = ref[:, pl.ds(i * HALF, HALF)]


def weight_kernel(own, x, far, y, out, whole, sems):
    core = lax.rem(lax.axis_index("dp"), 2)
    rows = own.shape[0] // PARTS
    copies = []
    for i in range(PARTS):
        block = pl.ds(i * rows, rows)
        for c, near, added in ((core, own, x), (1 - core, far, y)):
            for side in range(2):
                at = pl.ds(side * HALF, HALF)
                whole[block, ds(side * F + c * HALF, HALF, HALF)] = near[block, at] + added[block, at].astype(F32)
        copies.append(pltpu.make_async_copy(whole.at[block, :], out.at[block, :], sems.at[i]))
        copies[-1].start()
    for copy in copies:
        copy.wait()


def like(shape, kind):
    return jax.ShapeDtypeStruct(shape, kind)


def halve(terms, count):
    bit = count // 2
    while bit >= 8:
        terms = {
            m: (t.astype(F32) + pair(terms[m + bit], bit).astype(F32)).astype(BF) for m, t in terms.items() if m < bit
        }
        bit //= 2
    return terms


def on_device(inputs, values, gate_values, out_grad, lengths, qk_weight):
    count = lax.axis_size("dp")
    core = lax.rem(lax.axis_index("dp"), 2)
    xo, vo, go, grads = inputs[0, 0], values[0, 0], gate_values[0, 0], out_grad[0, 0]
    shard = qk_weight[0]
    rows, depth = shard.shape[0], xo.shape[1]
    seq_len = xo.shape[0]
    two = 2 * seq_len
    per = 256 // rows
    blocks = [tuple(range(b, b + per)) for b in range(0, count, per)]
    block = pltpu.VMEM((per * rows, F), BF)

    def half(x, c):
        return lax.dynamic_slice_in_dim(x, c * HALF, HALF, 1)

    def held(some):
        return [pieces[m] for masks in some for m in masks if m != 1]

    mine, other = (jnp.concatenate([half(shard[:, :F], c), half(shard[:, F:], c)], 1) for c in (core, 1 - core))
    bundle, vgo = call(
        pack_kernel, 0.001, [like((two + rows, F), BF), like((seq_len, F), BF)], other, xo, vo, go
    )
    pieces = {0: mine}
    pieces[2] = pair(mine, 2)
    pieces[5] = pair(other, 5)
    partner = pair(bundle, 1)
    cp = from_next(half(after(grads, partner), 1 - core), 1)
    co = from_next(half(grads, core))
    pieces[3] = pair(after(other, partner), 3)
    pieces[4] = pair(after(mine, partner), 4)
    xt = call(
        functools.partial(turn_kernel, count),
        10,
        like((depth, two), BF),
        bundle,
        partner,
        scratch=[pltpu.VMEM((depth, two), BF)],
    )
    pieces[6] = pair(after(pieces[2], xt), 4)
    pieces[7] = pair(after(pieces[5], xt), 2)
    pieces[1] = partner[two:]
    bit = 8
    while bit < count:
        for m in range(bit):
            pieces[m + bit] = pair(pieces[m], bit)
        bit *= 2
    first = functools.partial(pre_kernel, blocks[:1], False)
    pre = call(first, 0.001, like((two, F), F32), bundle, partner, *held(blocks[:1]), scratch=[block])
    more = functools.partial(pre_kernel, blocks[1:-1], True)
    pre = call(more, 10, like((two, F), F32), bundle, partner, after(pre, xt), *held(blocks[1:-1]), scratch=[block])
    co, cp, pre = lax.optimization_barrier((co, cp, pre))
    act, sigs, prob, prob_slope, mixed = call(
        functools.partial(forward_kernel, blocks[-1]),
        1,
        [
            like((two, F), BF),
            like((two, F), F32),
            like((2 * HL, seq_len, seq_len), BF),
            like((2 * HL, seq_len, seq_len), BF),
            like((two, HALF), F32),
        ],
        bundle,
        partner,
        pre,
        vgo,
        *held(blocks[-1:]),
        scratch=[block],
    )
    prod, stats = call(
        stats_kernel,
        0.1, [like((two, HALF), F32), like((8, two), F32)], lengths, mixed, vgo, partner, co, cp
    )
    theirs = pair(stats, 1)
    slope = call(slope_kernel, 0.3, like((two, F), F32), act, after(sigs, stats))

    far = [m for m in range(count) if m % 8 >= 6]
    near = [m for m in range(count) if m % 8 < 6]
    gpre, dmixed, *terms = call(
        functools.partial(backward_kernel, far),
        0.1,
        [like((two, F), BF), like((two, HALF), BF)] + [like((rows, F), BF)] * len(far),
        xt,
        act,
        slope,
        prob_slope,
        mixed,
        stats,
        theirs,
        vgo,
        partner,
        prod,
    )
    diagonal = halve(dict(zip(far, terms)), count)
    by_x, by_y = lax.optimization_barrier((pair(diagonal[6], 2), pair(diagonal[7], 4)))
    terms = call(functools.partial(term_kernel, near), 10, [like((rows, F), BF)] * len(near), xt, gpre)
    t = halve(dict(zip(near, terms)), count)
    own_g, far_g = call(
        grad_kernel, 3, [like((seq_len, F), BF)] * 2, prob, dmixed, mixed, stats, theirs, co, cp
    )
    far_g = pair(far_g, 1)
    x_r, y_r = lax.optimization_barrier((pair(t[2], 2), pair(t[5], 5)))
    far_t = pair(after(t[1], far_g), 1)
    near_own, near_far = call(near_kernel, 3, [like((rows, F), F32)] * 2, t[0], x_r, far_t, y_r)
    gi_o, gi_other = call(
        functools.partial(input_kernel, blocks),
        10,
        [like((seq_len, depth), F32), like((seq_len, depth), BF)],
        mine,
        partner,
        *held(blocks)[1:],
        gpre,
        scratch=[block],
    )
    gi_r = pair(after(gi_other, far_t), 1)
    send_y = call(fold_kernel, 0.3, like((rows, F), BF), t[4], by_x)
    send_x = call(fold_kernel, 0.3, like((rows, F), BF), t[3], by_y)
    grad_in, grad_val, grad_gate = call(
        collect_kernel, 0.3, [like((seq_len, F), BF)] * 3, gi_o, gi_r, own_g, far_g
    )
    sums = [near_own, pair(send_y, 4), near_far, pair(send_x, 3)]
    sums, _ = lax.optimization_barrier((sums, (grad_in, grad_val, grad_gate)))
    grad_shard = pl.pallas_call(
        weight_kernel,
        out_shape=like((rows, 2 * F), F32),
        in_specs=[VMEM] * 4,
        out_specs=pl.BlockSpec(memory_space=pl.ANY),
        scratch_shapes=[pltpu.VMEM((rows, 2 * F), F32), pltpu.SemaphoreType.DMA((PARTS,))],
        compiler_params=pltpu.CompilerParams(vmem_limit_bytes=20 << 20),
    )(*sums)
    return (grad_in[None, None], grad_val[None, None], grad_gate[None, None], grad_shard[None])


def solution(mesh):
    return jax.shard_map(
        on_device,
        mesh=mesh,
        in_specs=(
            P("segment", "dp", None, None),
            P("segment", "dp", None, None),
            P("segment", "dp", None, None),
            P("segment", "dp", None, None),
            P("segment", "dp"),
            P("segment", "dp", None),
        ),
        out_specs=(
            P("segment", "dp", None, None),
            P("segment", "dp", None, None),
            P("segment", "dp", None, None),
            P("segment", "dp", None),
        ),
        check_vma=False,
    )
```
